768 devices in a mesh: rows: 192 (over z, y, core), cols: 4 (over x).
Axes of the slice: x: 4, y: 8, z: 12, core: 2. Of those that a mesh axis runs over, the one named last changes fastest.
Arguments:
- features: bfloat16 [256, 393216], P('cols', 'rows'), may hold values from -6 to 6
- node_order: int32 [192, 2048], P('rows'), may hold values from 0 to 2047, each once within a row
- adj_values: bfloat16 [18432, 128, 128], P('rows'), may hold values from -0.3125 to 0.3125
- blk_dest: int32 [192, 96], P('rows'), may hold values from 0 to 15, as said below
- blk_src: int32 [192, 96], P('rows'), may hold values from 0 to 79, as said below
- blk_count: int32 [192], P('rows'), may hold values from 12 to 96, as said below
- weight: bfloat16 [256, 256], replicated, may hold values from -0.375 to 0.375
- bias: float32 [256], replicated, may hold values from -3 to 3
- cotangent: bfloat16 [256, 393216], P(None, ('rows', 'cols')), may hold values from -6 to 6
Outputs:
- output: bfloat16 [256, 393216], P(None, ('rows', 'cols'))
- grad_x: bfloat16 [256, 393216], P('cols', 'rows')
- grad_w: float32 [256, 256], replicated
- grad_b: float32 [256], replicated
The draws below stay inside these ranges and needn't reach their ends.
Inputs may be any that keep to these rules, and one draw needn't show every extreme that they name: `blk_dest`: destination block of a slot within its shard's 16 blocks. `blk_src`: Slot's source block (t + 2) * 16 + b: block b of shard (s + t) mod 192. Slots j < blk_count[s] are in use, the others are ignored; some shard has exactly 96 in use. Blocks may repeat.
All inputs are finite; a program needn't handle non-finite values.
Results may differ from the reference program's by a relative error of at most 0.01.
Values may be sent and summed in bfloat16 or wider, within the bound.
No kernel may reach another device: no remote copies, remote signals or barrier semaphores. Data moves between devices by JAX's collectives and lax.ppermute only.
A program may use at most 32 MiB of HBM per device.

```python
import math
import jax
import jax.numpy as jnp
from jax import lax

F_IN = 256
F_OUT = 256
BLOCK = 128
HOP = 2
NODE_DEV = 2048
NB = 16
MAX_BLOCKS = 96
WINDOW = 80
SHARDS = 192
NODES = 393216


def block_lists(key):
    subkeys = jax.random.split(key, 4)
    targets = jax.random.randint(subkeys[0], (SHARDS, MAX_BLOCKS), 0, NB, dtype=jnp.int32)
    sources = jax.random.randint(subkeys[1], (SHARDS, MAX_BLOCKS), 0, WINDOW, dtype=jnp.int32)
    halving = jax.random.randint(subkeys[2], (SHARDS,), 0, 4, dtype=jnp.int32)
    counts = jnp.right_shift(jnp.full((SHARDS,), MAX_BLOCKS, jnp.int32), halving)
    fullest = jax.random.randint(subkeys[3], (), 0, SHARDS, dtype=jnp.int32)
    counts = jnp.where(jnp.arange(SHARDS, dtype=jnp.int32) == fullest, jnp.int32(MAX_BLOCKS), counts)
    return (targets, sources, counts)


def draw_blk_dest(key, part):
    return block_lists(key)[0]


def draw_blk_src(key, part):
    return block_lists(key)[1]


def draw_blk_count(key, part):
    return block_lists(key)[2]


def level_of(rng, extent, cuts, smallest, largest):
    def one(dim, blocks):
        steps = jax.random.uniform(jax.random.fold_in(jax.random.fold_in(rng, 6), dim), (blocks,), jnp.float32, smallest / len(cuts), largest / len(cuts))
        return jnp.repeat(jnp.exp(steps), extent[dim] // blocks).reshape((-1,) + (1,) * (len(extent) - dim - 1))

    factor_of = one(*cuts[0])
    for cut in cuts[1:]:
        factor_of = factor_of * one(*cut)
    return factor_of


def bell_draw(own_key, shape, spread, most, shards=(), kind=jnp.bfloat16):
    loudness = level_of(own_key, shape, shards, -0.22, 0.18) if shards else 1.0
    result = jax.random.normal(own_key, shape, jnp.float32) * spread * loudness
    return jnp.minimum(jnp.maximum(result, -most), most).astype(kind)


def setup_inputs(seed: int = 0) -> dict:
    streams_of = jax.random.split(jax.random.key(seed), 10)
    features = bell_draw(streams_of[0], (F_IN, NODES), 1.0, 6.0, ((0, 4), (1, 192)))
    node_order = jax.vmap(lambda own: jax.random.permutation(own, NODE_DEV))(jax.random.split(streams_of[1], SHARDS)).reshape((SHARDS, NODE_DEV)).astype(jnp.int32)
    adj_values = bell_draw(streams_of[2], (SHARDS * MAX_BLOCKS, BLOCK, BLOCK), (3 * BLOCK) ** -0.5, 0.3125, ((0, 192),))
    blk_dest = draw_blk_dest(jax.random.fold_in(streams_of[9], 71), 0)
    blk_src = draw_blk_src(jax.random.fold_in(streams_of[9], 71), 0)
    blk_count = draw_blk_count(jax.random.fold_in(streams_of[9], 71), 0)
    weight = bell_draw(streams_of[6], (F_IN, F_OUT), F_IN ** -0.5, 0.375)
    bias = bell_draw(streams_of[7], (F_OUT,), 0.5, 3.0, (), jnp.float32)
    cotangent = bell_draw(streams_of[8], (F_OUT, NODES), 1.0, 6.0, ((1, 768),))
    return {"features": features, "node_order": node_order, "adj_values": adj_values, "blk_dest": blk_dest, "blk_src": blk_src, "blk_count": blk_count, "weight": weight, "bias": bias, "cotangent": cotangent}


def activation(values):
    return jax.nn.gelu(values, approximate=True)

def reference(features, node_order, adj_values, blk_dest, blk_src, blk_count, weight, bias, cotangent):
    width_in = features.shape[0]
    per_shard = features.reshape(width_in, SHARDS, NODE_DEV)
    permuted = jnp.take_along_axis(per_shard, node_order[None, :, :].astype(jnp.int32), axis=2)
    blocks = permuted.reshape(width_in, SHARDS, NB, BLOCK)
    spans = jnp.arange(-HOP, HOP + 1, dtype=jnp.int32)
    slot_ids = jnp.arange(MAX_BLOCKS, dtype=jnp.int32)
    block_ids = jnp.arange(NB, dtype=jnp.int32)
    window_ids = jnp.arange(WINDOW, dtype=jnp.int32)

    def forward_shard(shard):
        shard = shard.astype(jnp.int32)
        neighbours = (shard + spans) % SHARDS
        window = jnp.take(blocks, neighbours, axis=1).reshape(width_in, WINDOW, BLOCK)
        picked = jnp.take(window, blk_src[shard], axis=1)
        values = lax.dynamic_slice_in_dim(adj_values, (shard * MAX_BLOCKS).astype(jnp.int32), MAX_BLOCKS, 0)
        products = jnp.einsum('fjs,jds->jfd', picked.astype(jnp.float32), values.astype(jnp.float32))
        in_use = slot_ids < blk_count[shard]
        onehot = ((blk_dest[shard][None, :] == block_ids[:, None]) & in_use[None, :]).astype(jnp.float32)
        summed = jnp.einsum('bj,jfd->fbd', onehot, products, precision=lax.Precision.HIGHEST)
        return summed.reshape(width_in, NODE_DEV)
    hidden = lax.map(forward_shard, jnp.arange(SHARDS, dtype=jnp.int32))
    hidden = jnp.transpose(hidden, (1, 0, 2)).reshape(width_in, NODE_DEV * SHARDS).astype(jnp.bfloat16)
    preact = lax.dot_general(weight, hidden, (((0,), (0,)), ((), ())), preferred_element_type=jnp.float32) + bias[:, None]
    output, pullback = jax.vjp(activation, preact)
    grad_pre = pullback(cotangent.astype(jnp.float32))[0].astype(jnp.bfloat16)
    scale = 1.0 / math.sqrt(NODE_DEV * SHARDS)
    grad_w = lax.dot_general(hidden, grad_pre, (((1,), (1,)), ((), ())), preferred_element_type=jnp.float32) * scale
    grad_b = lax.optimization_barrier(jnp.sum(grad_pre.astype(jnp.float32), axis=1)) * scale
    grad_hidden = jnp.dot(weight, grad_pre, preferred_element_type=jnp.float32).astype(jnp.bfloat16)
    back_blocks = grad_hidden.reshape(width_in, SHARDS, NB, BLOCK)

    def backward_shard(shard, accumulated):
        shard = shard.astype(jnp.int32)
        local = jnp.take(back_blocks, shard, axis=1)
        picked = jnp.take(local, blk_dest[shard], axis=1)
        values = lax.dynamic_slice_in_dim(adj_values, (shard * MAX_BLOCKS).astype(jnp.int32), MAX_BLOCKS, 0)
        products = jnp.einsum('fjd,jds->jfs', picked.astype(jnp.float32), values.astype(jnp.float32))
        in_use = slot_ids < blk_count[shard]
        onehot = ((blk_src[shard][None, :] == window_ids[:, None]) & in_use[None, :]).astype(jnp.float32)
        onehot = onehot.reshape(2 * HOP + 1, NB, MAX_BLOCKS)
        parts = jnp.einsum('obj,jfs->ofbs', onehot, products, precision=lax.Precision.HIGHEST)
        parts = parts.reshape(2 * HOP + 1, width_in, NODE_DEV)
        for offset in range(2 * HOP + 1):
            target = ((shard + offset - HOP) % SHARDS).astype(jnp.int32)
            accumulated = accumulated.at[target].add(parts[offset])
        return accumulated
    accumulated = lax.fori_loop(0, SHARDS, backward_shard, jnp.zeros((SHARDS, width_in, NODE_DEV), jnp.float32))
    inverse = jnp.argsort(node_order, axis=1).astype(jnp.int32)
    grad_perm = jnp.transpose(accumulated, (1, 0, 2))
    grad_x = jnp.take_along_axis(grad_perm, inverse[None, :, :], axis=2)
    grad_x = grad_x.reshape(width_in, NODE_DEV * SHARDS).astype(jnp.bfloat16)
    return (output.astype(jnp.bfloat16), grad_x, grad_w, grad_b)
```

```python
import math

import jax
import jax.numpy as jnp
from jax import lax
from jax.experimental import pallas as pl
from jax.experimental.pallas import tpu as pltpu
from jax.sharding import Mesh, PartitionSpec as P

BF16 = jnp.bfloat16
F32 = jnp.float32
BLOCK = 128
TILE = 256
ROWS = ("z", "y", "c")
CHUNK = 8
VMEM = pl.BlockSpec(memory_space=pltpu.VMEM)
SMEM = pl.BlockSpec(memory_space=pltpu.SMEM)
ANY = pl.BlockSpec(memory_space=pl.ANY)
PARAMS = pltpu.CompilerParams(vmem_limit_bytes=40 * 1024 * 1024)


def into_order(order_ref, x_ref, out_ref):
    count = x_ref.shape[1]
    for start in range(0, count, TILE):
        rows = lax.broadcasted_iota(jnp.int32, (count, TILE), 0)
        hot = jnp.where(order_ref[:, start : start + TILE] == rows, 1.0, 0.0).astype(BF16)
        moved = jnp.dot(x_ref[...], hot, preferred_element_type=F32)
        out_ref[:, start : start + TILE] = moved.astype(BF16)


def out_of_order(order_ref, own_ref, near_ref, first_ref, second_ref, out_ref, total_ref):
    count = own_ref.shape[1]
    total = own_ref[...] + near_ref[...].astype(F32)
    total = total + first_ref[...].astype(F32) + second_ref[...].astype(F32)
    total_ref[...] = total.astype(BF16)
    for start in range(0, count, TILE):
        rows = lax.broadcasted_iota(jnp.int32, (TILE, count), 0) + start
        hot = jnp.where(order_ref[...] == rows, 1.0, 0.0).astype(BF16)
        moved = lax.dot_general(
            total_ref[...], hot, (((1,), (1,)), ((), ())), preferred_element_type=F32
        )
        out_ref[:, start : start + TILE] = moved.astype(BF16)


def mirrored(source, core, nblocks, spread):
    offset = source // nblocks
    return jnp.where(core == 0, offset, spread - 1 - offset), source % nblocks


def adjacency_copies(adj_ref, adj, sems):
    slots = adj.shape[0]
    copies = []
    for index, start in enumerate(range(0, slots, CHUNK)):
        part = pl.ds(start, CHUNK)
        copies.append(pltpu.make_async_copy(adj_ref.at[part], adj.at[part], sems.at[index]))
    return copies


def aggregate(
    dest_ref, src_ref, count_ref, core_ref, w0, w1, w2, w3, w4, adj_ref, out_ref, win, adj, acc, wsem, asem
):
    slots = adj.shape[0]
    nblocks = acc.shape[0] - 1
    spread = win.shape[0]
    quarter = out_ref.shape[2] // BLOCK
    win_copies = [
        pltpu.make_async_copy(ref, win.at[i], wsem.at[i])
        for i, ref in enumerate((w0, w1, w2, w3, w4))
    ]
    adj_copies = adjacency_copies(adj_ref, adj, asem)
    for copy in win_copies + adj_copies:
        copy.start()
    acc[...] = jnp.zeros_like(acc)
    for copy in win_copies:
        copy.wait()
    core = core_ref[0]
    count = count_ref[0]
    for index, copy in enumerate(adj_copies):
        copy.wait()
        products = []
        for j in range(index * CHUNK, (index + 1) * CHUNK):
            offset, block = mirrored(src_ref[0, j], core, nblocks, spread)
            picked = win[offset, :, pl.ds(pl.multiple_of(block * BLOCK, BLOCK), BLOCK)]
            products.append(
                lax.dot_general(
                    picked, adj[j], (((1,), (1,)), ((), ())), preferred_element_type=F32
                )
            )
        for j, product in zip(range(index * CHUNK, (index + 1) * CHUNK), products):
            target = jnp.where(j < count, dest_ref[0, j], nblocks)
            acc[target] += product
    for block in range(nblocks):
        lane = (block % quarter) * BLOCK
        out_ref[block // quarter, :, lane : lane + BLOCK] = acc[block].astype(BF16)


def dense(hidden_ref, weight_ref, bias_ref, cot_ref, out_ref, send_ref):
    feat, width = hidden_ref.shape
    part = send_ref.shape[0]
    rows = feat // part
    hidden = hidden_ref[...]
    weight = weight_ref[...]
    v = (
        lax.dot_general(weight, hidden, (((0,), (0,)), ((), ())), preferred_element_type=F32)
        + bias_ref[...]
    )
    root = math.sqrt(2.0 / math.pi)
    square = v * v
    t = jnp.tanh(root * (v + 0.044715 * (square * v)))
    half = 0.5 * (1.0 + t)
    out_ref[...] = (v * half).astype(BF16)
    slope = half + (0.5 * root) * v * (1.0 - t * t) * (1.0 + (3.0 * 0.044715) * square)
    grad = (cot_ref[...].astype(F32) * slope).astype(BF16)
    back = jnp.dot(weight, grad, preferred_element_type=F32).astype(BF16)
    grad_w = lax.dot_general(hidden, grad, (((1,), (1,)), ((), ())), preferred_element_type=F32)
    ones = jnp.ones((16, width), BF16)
    grad_b = lax.dot_general(ones, grad, (((1,), (1,)), ((), ())), preferred_element_type=F32)
    high_w = grad_w.astype(BF16)
    low_w = (grad_w - high_w.astype(F32)).astype(BF16)
    high_b = grad_b.astype(BF16)
    low_b = (grad_b - high_b.astype(F32)).astype(BF16)
    half_width = grad_w.shape[1]
    for i in range(part):
        span = slice(i * rows, (i + 1) * rows)
        send_ref[i, 0:rows, :] = back[span]
        send_ref[i, rows : 2 * rows, 0:half_width] = high_w[span]
        send_ref[i, rows : 2 * rows, half_width:] = low_w[span]
        send_ref[i, 2 * rows :, 0:half_width] = high_b
        send_ref[i, 2 * rows :, half_width:] = low_b


def first_sum(recv_ref, out_ref):
    part, height, width = recv_ref.shape
    rows = (height - 16) // 2
    half_width = width // 2
    total = jnp.zeros((rows + 16, half_width), F32)
    for i in range(part):
        total = total + recv_ref[i, rows:, 0:half_width].astype(F32)
        total = total + recv_ref[i, rows:, half_width:].astype(F32)
    pieces = out_ref.shape[0] // 2
    for i in range(pieces):
        for c in range(2):
            lane = slice(c * BLOCK, (c + 1) * BLOCK)
            out_ref[2 * i + c, 0:8, :] = total[8 * i : 8 * i + 8, lane]
            out_ref[2 * i + c, 8:12, :] = total[rows : rows + 4, 0:BLOCK]
            out_ref[2 * i + c, 12:16, :] = total[rows : rows + 4, BLOCK : 2 * BLOCK]


def spread_back(
    dest_ref, src_ref, count_ref, core_ref, recv_ref, adj_ref,
    first_ref, far_ref, near_ref, own_ref, last_ref, grad, adj, acc, gsem, asem,
):
    slots = adj.shape[0]
    rows = grad.shape[1]
    quarter = grad.shape[2] // BLOCK
    nblocks = grad.shape[0] * quarter
    spread = (acc.shape[0] - 1) // nblocks
    grad_copy = pltpu.make_async_copy(recv_ref.at[:, pl.ds(0, rows), :], grad, gsem)
    grad_copy.start()
    adj_copies = adjacency_copies(adj_ref, adj, asem)
    for copy in adj_copies:
        copy.start()
    acc[...] = jnp.zeros_like(acc)
    core = core_ref[0]
    count = count_ref[0]
    grad_copy.wait()
    for index, copy in enumerate(adj_copies):
        copy.wait()
        products = []
        for j in range(index * CHUNK, (index + 1) * CHUNK):
            target = dest_ref[0, j]
            lane = pl.multiple_of((target % quarter) * BLOCK, BLOCK)
            picked = grad[target // quarter, :, pl.ds(lane, BLOCK)]
            products.append(jnp.dot(picked, adj[j], preferred_element_type=F32))
        for j, product in zip(range(index * CHUNK, (index + 1) * CHUNK), products):
            offset, block = mirrored(src_ref[0, j], core, nblocks, spread)
            place = jnp.where(j < count, offset * nblocks + block, spread * nblocks)
            acc[place] += product
    for offset, ref in enumerate((first_ref, far_ref, own_ref, near_ref, last_ref)):
        for block in range(nblocks):
            lane = slice(block * BLOCK, (block + 1) * BLOCK)
            ref[:, lane] = acc[offset * nblocks + block].astype(ref.dtype)


def on_device(
    features, node_order, adj_values, blk_dest, blk_src, blk_count, weight, bias, cotangent
):
    feat, nodes = features.shape
    slots = adj_values.shape[0]
    nblocks = nodes // BLOCK
    parts = lax.axis_size("x")
    out_feat, width = cotangent.shape
    shards = lax.axis_size(ROWS)
    ys, zs = lax.axis_size("y"), lax.axis_size("z")
    core = lax.axis_index("c").astype(jnp.int32).reshape(1)
    scale = 1.0 / math.sqrt(nodes * shards)

    def chip_step(value, sign):
        pairs = [(s, (s + (2 * sign if s % 2 == 0 else -2 * sign)) % shards) for s in range(shards)]
        return lax.ppermute(value, ROWS, pairs)

    def sibling(value):
        return lax.ppermute(value, "c", [(0, 1), (1, 0)])

    permuted = pl.pallas_call(
        into_order,
        out_shape=jax.ShapeDtypeStruct((feat, nodes), BF16),
        in_specs=[VMEM, VMEM],
        out_specs=VMEM,
        compiler_params=PARAMS,
        name="into_order",
    )(node_order, features)

    after = chip_step(permuted, -1)
    before = chip_step(permuted, 1)
    beside = sibling(permuted)
    across = sibling(after)

    hidden = pl.pallas_call(
        aggregate,
        out_shape=jax.ShapeDtypeStruct((parts, feat, width), BF16),
        in_specs=[SMEM] * 4 + [ANY] * 6,
        out_specs=VMEM,
        scratch_shapes=[
            pltpu.VMEM((5, feat, nodes), BF16),
            pltpu.VMEM((slots, BLOCK, BLOCK), BF16),
            pltpu.VMEM((nblocks + 1, feat, BLOCK), F32),
            pltpu.SemaphoreType.DMA((5,)),
            pltpu.SemaphoreType.DMA((slots // CHUNK,)),
        ],
        compiler_params=PARAMS,
        name="aggregate",
    )(blk_dest, blk_src, blk_count, core, before, across, permuted, beside, after, adj_values)

    hidden_rows = lax.all_to_all(hidden, "x", 0, 0).reshape(parts * feat, width)

    output, send = pl.pallas_call(
        dense,
        out_shape=(
            jax.ShapeDtypeStruct((out_feat, width), BF16),
            jax.ShapeDtypeStruct((parts, 2 * feat + 16, width), BF16),
        ),
        in_specs=[VMEM] * 4,
        out_specs=(VMEM, VMEM),
        compiler_params=PARAMS,
        name="dense",
    )(hidden_rows, weight, bias[:, None], cotangent)

    recv = lax.all_to_all(send, "x", 0, 0)

    partial = pl.pallas_call(
        first_sum,
        out_shape=jax.ShapeDtypeStruct((2 * ys, 16, BLOCK), F32),
        in_specs=[VMEM],
        out_specs=VMEM,
        compiler_params=PARAMS,
        name="first_sum",
    )(recv)
    partial = lax.all_to_all(partial, ("y", "c"), 0, 0)
    partial = jnp.sum(partial, axis=0)
    partial = lax.all_to_all(jnp.broadcast_to(partial[None], (zs, 16, BLOCK)), "z", 0, 0)
    partial = jnp.sum(partial, axis=0) * scale
    grad_b = jnp.concatenate([partial[8], partial[12]])
    pieces = lax.all_to_all(jnp.broadcast_to(partial[None, 0:8], (2 * ys, 8, BLOCK)), ("y", "c"), 0, 0)
    pieces = pieces.reshape(ys, 2, 8, BLOCK).transpose(0, 2, 1, 3).reshape(8 * ys, 2 * BLOCK)
    grad_w = lax.all_to_all(jnp.broadcast_to(pieces[None], (parts,) + pieces.shape), "x", 0, 0)
    grad_w = grad_w.reshape(parts * 8 * ys, 2 * BLOCK)

    half = jax.ShapeDtypeStruct((feat, nodes), BF16)
    whole = jax.ShapeDtypeStruct((feat, nodes), F32)
    first, far, near, own, last = pl.pallas_call(
        spread_back,
        out_shape=(half, half, half, whole, whole),
        in_specs=[SMEM] * 4 + [ANY] * 2,
        out_specs=(VMEM,) * 5,
        scratch_shapes=[
            pltpu.VMEM((parts, feat, width), BF16),
            pltpu.VMEM((slots, BLOCK, BLOCK), BF16),
            pltpu.VMEM((5 * nblocks + 1, feat, BLOCK), F32),
            pltpu.SemaphoreType.DMA,
            pltpu.SemaphoreType.DMA((slots // CHUNK,)),
        ],
        compiler_params=PARAMS,
        name="spread_back",
    )(blk_dest, blk_src, blk_count, core, recv, adj_values)

    from_first = chip_step(first, -1)
    far = sibling(far)
    near = sibling(near)
    from_last = chip_step((last + far.astype(F32)).astype(BF16), 1)

    grad_x = pl.pallas_call(
        out_of_order,
        out_shape=jax.ShapeDtypeStruct((feat, nodes), BF16),
        in_specs=[VMEM] * 5,
        out_specs=VMEM,
        scratch_shapes=[pltpu.VMEM((feat, nodes), BF16)],
        compiler_params=PARAMS,
        name="out_of_order",
    )(node_order, own, near, from_first, from_last)
    return output, grad_x, grad_w, grad_b


def solution(mesh):
    rows, cols = mesh.devices.shape
    ys = 8 if rows % 16 == 0 else 2
    devices = mesh.devices.reshape(rows // (2 * ys), ys, 2, cols)
    own = Mesh(devices, ("z", "y", "c", "x"))
    in_specs = (
        P("x", ROWS),
        P(ROWS, None),
        P(ROWS, None, None),
        P(ROWS, None),
        P(ROWS, None),
        P(ROWS),
        P(),
        P(),
        P(None, ROWS + ("x",)),
    )
    out_specs = (P(None, ROWS + ("x",)), P("x", ROWS), P(), P())
    return jax.shard_map(
        on_device, mesh=own, in_specs=in_specs, out_specs=out_specs, check_vma=False
    )
```

```python
import math

import jax
import jax.numpy as jnp
from jax import lax
from jax.experimental import pallas as pl
from jax.experimental.pallas import tpu as pltpu
from jax.sharding import Mesh, PartitionSpec as P

BF16 = jnp.bfloat16
F32 = jnp.float32
BLOCK = 128
TILE = 256
ROWS = ("z", "y", "c")
CHUNK = 8
VMEM = pl.BlockSpec(memory_space=pltpu.VMEM)
SMEM = pl.BlockSpec(memory_space=pltpu.SMEM)
HBM = pl.BlockSpec(memory_space=pltpu.HBM)
ANY = pl.BlockSpec(memory_space=pl.ANY)
PARAMS = pltpu.CompilerParams(vmem_limit_bytes=40 * 1024 * 1024)


def in_hbm(*arrays):
    return tuple(pltpu.with_memory_space_constraint(array, pltpu.HBM) for array in arrays)


def cost(flops, size):
    return pl.CostEstimate(flops=flops, bytes_accessed=size, transcendentals=0)


def started(pairs, sems):
    copies = [pltpu.make_async_copy(a, b, sems.at[i]) for i, (a, b) in enumerate(pairs)]
    for copy in copies:
        copy.start()
    return copies


def into_order(order_hbm, x_hbm, adj_hbm, out_ref, adj_ref, order, x, sems):
    copies = started([(x_hbm, x), (order_hbm, order), (adj_hbm, adj_ref)], sems)
    copies[0].wait()
    copies[1].wait()
    count = x.shape[1]
    for start in range(0, count, TILE):
        rows = lax.broadcasted_iota(jnp.int32, (count, TILE), 0)
        hot = jnp.where(order[:, start : start + TILE] == rows, 1.0, 0.0).astype(BF16)
        moved = jnp.dot(x[...], hot, preferred_element_type=F32)
        out_ref[:, start : start + TILE] = moved.astype(BF16)
    copies[2].wait()


def out_of_order(
    order_hbm, own_hbm, first_hbm, pair_hbm, last_hbm, out_ref, order, own, first, near, last, total, sems
):
    copies = started(
        [
            (last_hbm, last),
            (first_hbm, first),
            (pair_hbm.at[1], near),
            (own_hbm, own),
            (order_hbm, order),
        ],
        sems,
    )
    for copy in copies:
        copy.wait()
    count = own.shape[1]
    sums = own[...] + near[...].astype(F32) + first[...].astype(F32) + last[...].astype(F32)
    total[...] = sums.astype(BF16)
    for start in range(0, count, TILE):
        rows = lax.broadcasted_iota(jnp.int32, (TILE, count), 0) + start
        hot = jnp.where(order[...] == rows, 1.0, 0.0).astype(BF16)
        moved = lax.dot_general(
            total[...], hot, (((1,), (1,)), ((), ())), preferred_element_type=F32
        )
        out_ref[:, start : start + TILE] = moved.astype(BF16)


def mirrored(source, core, nblocks, spread):
    offset = source // nblocks
    return jnp.where(core == 0, offset, spread - 1 - offset), source % nblocks


def aggregate(
    count_ref, dest_hbm, src_hbm, w0, w1, w2, w3, w4, adj, out_ref, dest, src, win, acc, sems
):
    slots = adj.shape[0]
    nblocks = acc.shape[0] - 1
    spread = win.shape[0]
    quarter = out_ref.shape[2] // BLOCK
    windows = [(ref, win.at[i]) for i, ref in enumerate((w0, w1, w2, w3, w4))]
    copies = started([(dest_hbm, dest), (src_hbm, src)] + windows, sems)
    acc[...] = jnp.zeros_like(acc)
    for copy in copies:
        copy.wait()
    core = lax.axis_index("c")
    count = count_ref[0]
    for begin in range(0, slots, CHUNK):
        products = []
        for j in range(begin, begin + CHUNK):
            offset, block = mirrored(src[0, j], core, nblocks, spread)
            picked = win[offset, :, pl.ds(pl.multiple_of(block * BLOCK, BLOCK), BLOCK)]
            products.append(
                lax.dot_general(
                    picked, adj[j], (((1,), (1,)), ((), ())), preferred_element_type=F32
                )
            )
        for j, product in zip(range(begin, begin + CHUNK), products):
            target = jnp.where(j < count, dest[0, j], nblocks)
            acc[target] += product
    for block in range(nblocks):
        lane = (block % quarter) * BLOCK
        out_ref[block // quarter, :, lane : lane + BLOCK] = acc[block].astype(BF16)


def dense(hidden_ref, weight_hbm, bias_hbm, cot_hbm, out_ref, send_ref, weight_v, bias_v, cot, sems):
    copies = started([(weight_hbm, weight_v), (bias_hbm, bias_v), (cot_hbm, cot)], sems)
    feat, width = hidden_ref.shape
    part = send_ref.shape[0]
    rows = feat // part
    hidden = hidden_ref[...]
    copies[0].wait()
    copies[1].wait()
    weight = weight_v[...]
    bias = jnp.broadcast_to(bias_v[...], (BLOCK, bias_v.shape[1])).T
    bias = jnp.concatenate([bias] * (width // BLOCK), axis=1)
    v = (
        lax.dot_general(weight, hidden, (((0,), (0,)), ((), ())), preferred_element_type=F32)
        + bias
    )
    root = math.sqrt(2.0 / math.pi)
    square = v * v
    t = jnp.tanh(root * (v + 0.044715 * (square * v)))
    half = 0.5 * (1.0 + t)
    out_ref[...] = (v * half).astype(BF16)
    slope = half + (0.5 * root) * v * (1.0 - t * t) * (1.0 + (3.0 * 0.044715) * square)
    copies[2].wait()
    grad = (cot[...].astype(F32) * slope).astype(BF16)
    back = jnp.dot(weight, grad, preferred_element_type=F32).astype(BF16)
    grad_w = lax.dot_general(hidden, grad, (((1,), (1,)), ((), ())), preferred_element_type=F32)
    ones = jnp.ones((16, width), BF16)
    grad_b = lax.dot_general(ones, grad, (((1,), (1,)), ((), ())), preferred_element_type=F32)
    high_w = grad_w.astype(BF16)
    low_w = (grad_w - high_w.astype(F32)).astype(BF16)
    high_b = grad_b.astype(BF16)
    low_b = (grad_b - high_b.astype(F32)).astype(BF16)
    half_width = grad_w.shape[1]
    for i in range(part):
        span = slice(i * rows, (i + 1) * rows)
        send_ref[i, 0:rows, :] = back[span]
        send_ref[i, rows : 2 * rows, 0:half_width] = high_w[span]
        send_ref[i, rows : 2 * rows, half_width:] = low_w[span]
        send_ref[i, 2 * rows :, 0:half_width] = high_b
        send_ref[i, 2 * rows :, half_width:] = low_b


def first_sum(recv_hbm, out_hbm, recv, out, sems):
    rows = recv.shape[1] - 16
    half_width = recv.shape[2] // 2
    started([(recv_hbm.at[:, pl.ds(rows, rows + 16), :], recv)], sems)[0].wait()
    total = jnp.zeros((rows + 16, half_width), F32)
    for i in range(recv.shape[0]):
        total = total + recv[i, :, 0:half_width].astype(F32)
        total = total + recv[i, :, half_width:].astype(F32)
    for i in range(out.shape[0] // 2):
        for c in range(2):
            lane = slice(c * BLOCK, (c + 1) * BLOCK)
            out[2 * i + c, 0:8, :] = total[8 * i : 8 * i + 8, lane]
            out[2 * i + c, 8:12, :] = total[rows : rows + 4, 0:BLOCK]
            out[2 * i + c, 12:16, :] = total[rows : rows + 4, BLOCK : 2 * BLOCK]
    started([(out, out_hbm)], sems)[0].wait()


def spread_back(
    count_ref, dest_hbm, src_hbm, recv_hbm, adj_hbm,
    first_hbm, pair_hbm, own_hbm, last_hbm, token_ref,
    dest, src, grad, adj, acc, first, pair, own, last, sems, adj_sems,
):
    slots = adj.shape[0]
    rows = grad.shape[1]
    quarter = grad.shape[2] // BLOCK
    nblocks = grad.shape[0] * quarter
    spread = (acc.shape[0] - 1) // nblocks
    copies = started(
        [(dest_hbm, dest), (src_hbm, src), (recv_hbm.at[:, pl.ds(0, rows), :], grad)], sems
    )
    spans = [pl.ds(begin, CHUNK) for begin in range(0, slots, CHUNK)]
    adj_copies = started([(adj_hbm.at[span], adj.at[span]) for span in spans], adj_sems)
    acc[...] = jnp.zeros_like(acc)
    core = lax.axis_index("c")
    count = count_ref[0]
    for copy in copies:
        copy.wait()
    for index, copy in enumerate(adj_copies):
        copy.wait()
        products = []
        for j in range(index * CHUNK, (index + 1) * CHUNK):
            target = dest[0, j]
            lane = pl.multiple_of((target % quarter) * BLOCK, BLOCK)
            picked = grad[target // quarter, :, pl.ds(lane, BLOCK)]
            products.append(jnp.dot(picked, adj[j], preferred_element_type=F32))
        for j, product in zip(range(index * CHUNK, (index + 1) * CHUNK), products):
            offset, block = mirrored(src[0, j], core, nblocks, spread)
            place = jnp.where(j < count, offset * nblocks + block, spread * nblocks)
            acc[place] += product
    outs = []
    for offset, ref, target in (
        (1, pair.at[0], None),
        (3, pair.at[1], pair_hbm),
        (0, first, first_hbm),
        (4, last, last_hbm),
        (2, own, own_hbm),
    ):
        for block in range(nblocks):
            lane = slice(block * BLOCK, (block + 1) * BLOCK)
            ref[:, lane] = acc[offset * nblocks + block].astype(ref.dtype)
        if target is not None:
            source = pair if target is pair_hbm else ref
            copy = pltpu.make_async_copy(source, target, sems.at[3 + len(outs)])
            copy.start()
            outs.append(copy)
    token_ref[...] = jnp.zeros_like(token_ref)
    for copy in outs:
        copy.wait()


def on_device(
    features, node_order, adj_values, blk_dest, blk_src, blk_count, weight, bias, cotangent
):
    feat, nodes = features.shape
    slots = adj_values.shape[0]
    nblocks = nodes // BLOCK
    parts = lax.axis_size("x")
    out_feat, width = cotangent.shape
    shards = lax.axis_size(ROWS)
    ys, zs = lax.axis_size("y"), lax.axis_size("z")
    scale = 1.0 / math.sqrt(nodes * shards)

    def chip_step(value, sign):
        pairs = [(s, (s + (2 * sign if s % 2 == 0 else -2 * sign)) % shards) for s in range(shards)]
        return lax.ppermute(value, ROWS, pairs)

    def sibling(value):
        return lax.ppermute(value, "c", [(0, 1), (1, 0)])

    slab = jax.ShapeDtypeStruct((feat, nodes), BF16)
    dma = pltpu.SemaphoreType.DMA

    permuted, adj = pl.pallas_call(
        into_order,
        out_shape=(slab, jax.ShapeDtypeStruct(adj_values.shape, BF16)),
        in_specs=[HBM] * 3,
        out_specs=(VMEM, VMEM),
        scratch_shapes=[
            pltpu.VMEM((1, nodes), jnp.int32),
            pltpu.VMEM((feat, nodes), BF16),
            dma((3,)),
        ],
        compiler_params=PARAMS,
        cost_estimate=cost(10**9, 2**20),
        name="into_order",
    )(*in_hbm(node_order, features, adj_values))

    after = chip_step(permuted, -1)
    before = chip_step(permuted, 1)
    beside = sibling(permuted)
    across = sibling(after)

    hidden = pl.pallas_call(
        aggregate,
        out_shape=jax.ShapeDtypeStruct((parts, feat, width), BF16),
        in_specs=[SMEM] + [HBM] * 2 + [VMEM] * 6,
        out_specs=VMEM,
        scratch_shapes=[
            pltpu.SMEM((1, slots), jnp.int32),
            pltpu.SMEM((1, slots), jnp.int32),
            pltpu.VMEM((5, feat, nodes), BF16),
            pltpu.VMEM((nblocks + 1, feat, BLOCK), F32),
            dma((7,)),
        ],
        compiler_params=PARAMS,
        cost_estimate=cost(4 * 10**9, 2**22),
        name="aggregate",
    )(blk_count, *in_hbm(blk_dest, blk_src), before, across, permuted, beside, after, adj)

    hidden_rows = lax.all_to_all(hidden, "x", 0, 0).reshape(parts * feat, width)

    output, send = pl.pallas_call(
        dense,
        out_shape=(
            jax.ShapeDtypeStruct((out_feat, width), BF16),
            jax.ShapeDtypeStruct((parts, 2 * feat + 16, width), BF16),
        ),
        in_specs=[VMEM] + [HBM] * 3,
        out_specs=(VMEM, VMEM),
        scratch_shapes=[
            pltpu.VMEM(weight.shape, BF16),
            pltpu.VMEM((1, out_feat), F32),
            pltpu.VMEM((out_feat, width), BF16),
            dma((3,)),
        ],
        compiler_params=PARAMS,
        cost_estimate=cost(10**9, 2**20),
        name="dense",
    )(hidden_rows, *in_hbm(weight, bias[None, :], cotangent))

    recv = lax.all_to_all(send, "x", 0, 0)

    partial = pl.pallas_call(
        first_sum,
        out_shape=pltpu.HBM((2 * ys, 16, BLOCK), F32),
        in_specs=[HBM],
        out_specs=HBM,
        scratch_shapes=[
            pltpu.VMEM((parts, feat + 16, width), BF16),
            pltpu.VMEM((2 * ys, 16, BLOCK), F32),
            dma((1,)),
        ],
        compiler_params=PARAMS,
        cost_estimate=cost(10**9, 2**20),
        name="first_sum",
    )(*in_hbm(recv))
    partial = lax.all_to_all(partial, ("y", "c"), 0, 0)

    first, pair, own, last, token = pl.pallas_call(
        spread_back,
        out_shape=(
            pltpu.HBM((feat, nodes), BF16),
            pltpu.HBM((2, feat, nodes), BF16),
            pltpu.HBM((feat, nodes), F32),
            pltpu.HBM((feat, nodes), F32),
            jax.ShapeDtypeStruct((8, BLOCK), F32),
        ),
        in_specs=[SMEM] + [HBM] * 4,
        out_specs=(HBM,) * 4 + (VMEM,),
        scratch_shapes=[
            pltpu.SMEM((1, slots), jnp.int32),
            pltpu.SMEM((1, slots), jnp.int32),
            pltpu.VMEM((parts, feat, width), BF16),
            pltpu.VMEM((slots, BLOCK, BLOCK), BF16),
            pltpu.VMEM((5 * nblocks + 1, feat, BLOCK), F32),
            pltpu.VMEM((feat, nodes), BF16),
            pltpu.VMEM((2, feat, nodes), BF16),
            pltpu.VMEM((feat, nodes), F32),
            pltpu.VMEM((feat, nodes), F32),
            dma((7,)),
            dma((slots // CHUNK,)),
        ],
        compiler_params=PARAMS,
        cost_estimate=cost(4 * 10**9, 2**22),
        name="spread_back",
    )(blk_count, *in_hbm(blk_dest, blk_src, recv, adj_values))

    pair = sibling(pair)
    from_first = chip_step(first, -1)
    last = (last + pair[0].astype(F32)).astype(BF16)
    from_last = chip_step(last, 1)

    partial = lax.optimization_barrier((jnp.sum(partial, axis=0), token))[0]
    partial = lax.all_to_all(jnp.broadcast_to(partial[None], (zs, 16, BLOCK)), "z", 0, 0)
    partial = lax.optimization_barrier((jnp.sum(partial, axis=0) * scale, last))[0]
    grad_b = jnp.concatenate([partial[8], partial[12]])
    pieces = lax.all_to_all(jnp.broadcast_to(partial[None, 0:8], (2 * ys, 8, BLOCK)), ("y", "c"), 0, 0)
    pieces = pieces.reshape(ys, 2, 8, BLOCK).transpose(0, 2, 1, 3).reshape(8 * ys, 2 * BLOCK)
    grad_w = lax.all_to_all(jnp.broadcast_to(pieces[None], (parts,) + pieces.shape), "x", 0, 0)
    grad_w = grad_w.reshape(parts * 8 * ys, 2 * BLOCK)

    grad_x = pl.pallas_call(
        out_of_order,
        out_shape=slab,
        in_specs=[HBM] * 2 + [ANY] * 3,
        out_specs=VMEM,
        scratch_shapes=[
            pltpu.VMEM((1, nodes), jnp.int32),
            pltpu.VMEM((feat, nodes), F32),
            pltpu.VMEM((feat, nodes), BF16),
            pltpu.VMEM((feat, nodes), BF16),
            pltpu.VMEM((feat, nodes), BF16),
            pltpu.VMEM((feat, nodes), BF16),
            dma((5,)),
        ],
        compiler_params=PARAMS,
        cost_estimate=cost(3 * 10**9, 2**21),
        name="out_of_order",
    )(*in_hbm(node_order, own), from_first, pair, from_last)
    return output, grad_x, grad_w, grad_b


def solution(mesh):
    rows, cols = mesh.devices.shape
    ys = 8 if rows % 16 == 0 else 2
    devices = mesh.devices.reshape(rows // (2 * ys), ys, 2, cols)
    own = Mesh(devices, ("z", "y", "c", "x"))
    in_specs = (
        P("x", ROWS),
        P(ROWS, None),
        P(ROWS, None, None),
        P(ROWS, None),
        P(ROWS, None),
        P(ROWS),
        P(),
        P(),
        P(None, ROWS + ("x",)),
    )
    out_specs = (P(None, ROWS + ("x",)), P("x", ROWS), P(), P())
    return jax.shard_map(
        on_device, mesh=own, in_specs=in_specs, out_specs=out_specs, check_vma=False
    )
```

```python
import functools
import math

import jax
import jax.numpy as jnp
from jax import lax
from jax.experimental import pallas as pl
from jax.experimental.pallas import tpu as pltpu
from jax.sharding import Mesh, PartitionSpec as P

BF16 = jnp.bfloat16
F32 = jnp.float32
BLOCK = 128
TILE = 256
ROWS = ("z", "y", "c")
CHUNK = 8
VMEM = pl.BlockSpec(memory_space=pltpu.VMEM)
SMEM = pl.BlockSpec(memory_space=pltpu.SMEM)
HBM = pl.BlockSpec(memory_space=pltpu.HBM)
ANY = pl.BlockSpec(memory_space=pl.ANY)
PARAMS = pltpu.CompilerParams(vmem_limit_bytes=40 * 1024 * 1024)


def in_hbm(*arrays):
    return tuple(pltpu.with_memory_space_constraint(array, pltpu.HBM) for array in arrays)


def cost(flops, size):
    return pl.CostEstimate(flops=flops, bytes_accessed=size, transcendentals=0)


def started(pairs, sems):
    copies = [pltpu.make_async_copy(a, b, sems.at[i]) for i, (a, b) in enumerate(pairs)]
    for copy in copies:
        copy.start()
    return copies


def into_order(order_hbm, x_hbm, adj_hbm, out_ref, adj_ref, order, x, sems):
    copies = started([(x_hbm, x), (order_hbm, order), (adj_hbm, adj_ref)], sems)
    copies[0].wait()
    copies[1].wait()
    count = x.shape[1]
    for start in range(0, count, TILE):
        rows = lax.broadcasted_iota(jnp.int32, (count, TILE), 0)
        hot = jnp.where(order[:, start : start + TILE] == rows, 1.0, 0.0).astype(BF16)
        moved = jnp.dot(x[...], hot, preferred_element_type=F32)
        out_ref[:, start : start + TILE] = moved.astype(BF16)
    copies[2].wait()


def out_of_order(
    order_hbm, own_hbm, first_hbm, pair_hbm, last_hbm, out_ref, token_ref, order, own, first, near, last, total, sems
):
    copies = started(
        [
            (last_hbm, last),
            (first_hbm, first),
            (pair_hbm.at[1], near),
            (own_hbm, own),
            (order_hbm, order),
        ],
        sems,
    )
    token_ref[...] = jnp.zeros_like(token_ref)
    for copy in copies:
        copy.wait()
    for block in range(own.shape[0]):
        sums = own[block] + near[block].astype(F32)
        sums = sums + first[block].astype(F32) + last[block].astype(F32)
        total[:, block * BLOCK : (block + 1) * BLOCK] = sums.astype(BF16)
    count = total.shape[1]
    for start in range(0, count, TILE):
        rows = lax.broadcasted_iota(jnp.int32, (TILE, count), 0) + start
        hot = jnp.where(order[...] == rows, 1.0, 0.0).astype(BF16)
        moved = lax.dot_general(
            total[...], hot, (((1,), (1,)), ((), ())), preferred_element_type=F32
        )
        out_ref[:, start : start + TILE] = moved.astype(BF16)


def sum_to_all(recv, first_hbm, token, out_hbm, kept_hbm, out, sems):
    total = jnp.sum(recv[...], axis=0)
    for i in range(out.shape[0]):
        out[i] = total
    started([(out, out_hbm)], sems)[0].wait()


def last_sum(scale, recv, own_hbm, token, out_hbm, kept_hbm, bias_ref, out, sems):
    total = jnp.sum(recv[...], axis=0) * scale
    for i in range(out.shape[0]):
        out[i] = total[0:8]
    copies = started([(out, out_hbm)], sems)
    bias_ref[:, 0:BLOCK] = total[8:9]
    bias_ref[:, BLOCK:] = total[12:13]
    copies[0].wait()


def put_together(recv, token, out_hbm, out, sems):
    for i in range(recv.shape[0] // 2):
        for c in range(2):
            out[8 * i : 8 * i + 8, c * BLOCK : (c + 1) * BLOCK] = recv[2 * i + c]
    pairs = [(out, out_hbm.at[i]) for i in range(out_hbm.shape[0])]
    for copy in started(pairs, sems):
        copy.wait()


def mirrored(source, core, nblocks, spread):
    offset = source // nblocks
    return jnp.where(core == 0, offset, spread - 1 - offset), source % nblocks


def aggregate(
    count_ref, dest_hbm, src_hbm, before, across, permuted, beside, after, adj, out_ref, dest, src, win, acc, sems
):
    slots = adj.shape[0]
    nblocks = acc.shape[0] - 1
    spread = win.shape[0] // nblocks
    quarter = out_ref.shape[2] // BLOCK
    copies = started([(dest_hbm, dest), (src_hbm, src)], sems)
    acc[...] = jnp.zeros_like(acc)
    for block in range(nblocks):
        lane = slice(block * BLOCK, (block + 1) * BLOCK)
        win[block] = before[:, lane]
        win[nblocks + block] = across[:, lane]
        win[2 * nblocks + block] = permuted[:, lane]
        win[3 * nblocks + block] = beside[:, lane]
        win[4 * nblocks + block] = after[:, lane]
    core = lax.axis_index("c")
    count = count_ref[0]
    for copy in copies:
        copy.wait()
    for begin in range(0, slots, CHUNK):
        products = []
        for j in range(begin, begin + CHUNK):
            offset, block = mirrored(src[0, j], core, nblocks, spread)
            products.append(
                lax.dot_general(
                    win[offset * nblocks + block],
                    adj[j],
                    (((1,), (1,)), ((), ())),
                    preferred_element_type=F32,
                )
            )
        for j, product in zip(range(begin, begin + CHUNK), products):
            target = jnp.where(j < count, dest[0, j], nblocks)
            acc[target] += product
    for block in range(nblocks):
        lane = (block % quarter) * BLOCK
        out_ref[block // quarter, :, lane : lane + BLOCK] = acc[block].astype(BF16)


def dense(hidden_ref, weight_hbm, bias_hbm, cot_hbm, out_ref, send_ref, weight_v, bias_v, cot, sems):
    copies = started([(weight_hbm, weight_v), (bias_hbm, bias_v), (cot_hbm, cot)], sems)
    feat, width = hidden_ref.shape
    part = send_ref.shape[0]
    rows = feat // part
    hidden = hidden_ref[...]
    copies[0].wait()
    copies[1].wait()
    weight = weight_v[...]
    bias = jnp.broadcast_to(bias_v[...], (BLOCK, bias_v.shape[1])).T
    bias = jnp.concatenate([bias] * (width // BLOCK), axis=1)
    v = (
        lax.dot_general(weight, hidden, (((0,), (0,)), ((), ())), preferred_element_type=F32)
        + bias
    )
    root = math.sqrt(2.0 / math.pi)
    square = v * v
    t = jnp.tanh(root * (v + 0.044715 * (square * v)))
    half = 0.5 * (1.0 + t)
    out_ref[...] = (v * half).astype(BF16)
    slope = half + (0.5 * root) * v * (1.0 - t * t) * (1.0 + (3.0 * 0.044715) * square)
    copies[2].wait()
    grad = (cot[...].astype(F32) * slope).astype(BF16)
    back = jnp.dot(weight, grad, preferred_element_type=F32).astype(BF16)
    grad_w = lax.dot_general(hidden, grad, (((1,), (1,)), ((), ())), preferred_element_type=F32)
    ones = jnp.ones((16, width), BF16)
    grad_b = lax.dot_general(ones, grad, (((1,), (1,)), ((), ())), preferred_element_type=F32)
    high_w = grad_w.astype(BF16)
    low_w = (grad_w - high_w.astype(F32)).astype(BF16)
    high_b = grad_b.astype(BF16)
    low_b = (grad_b - high_b.astype(F32)).astype(BF16)
    half_width = grad_w.shape[1]
    for i in range(part):
        span = slice(i * rows, (i + 1) * rows)
        send_ref[i, 0:rows, :] = back[span]
        send_ref[i, rows : 2 * rows, 0:half_width] = high_w[span]
        send_ref[i, rows : 2 * rows, half_width:] = low_w[span]
        send_ref[i, 2 * rows :, 0:half_width] = high_b
        send_ref[i, 2 * rows :, half_width:] = low_b


def first_sum(recv, out_hbm, grad_hbm, out, sems):
    rows = grad_hbm.shape[1]
    half_width = recv.shape[2] // 2
    copies = started([(recv.at[:, pl.ds(0, rows), :], grad_hbm)], sems)
    total = jnp.zeros((rows + 16, half_width), F32)
    for i in range(recv.shape[0]):
        total = total + recv[i, rows:, 0:half_width].astype(F32)
        total = total + recv[i, rows:, half_width:].astype(F32)
    for i in range(out.shape[0] // 2):
        for c in range(2):
            lane = slice(c * BLOCK, (c + 1) * BLOCK)
            out[2 * i + c, 0:8, :] = total[8 * i : 8 * i + 8, lane]
            out[2 * i + c, 8:12, :] = total[rows : rows + 4, 0:BLOCK]
            out[2 * i + c, 12:16, :] = total[rows : rows + 4, BLOCK : 2 * BLOCK]
    last = pltpu.make_async_copy(out, out_hbm, sems.at[1])
    last.start()
    copies[0].wait()
    last.wait()


def spread_back(
    count_ref, dest_hbm, src_hbm, grad_hbm, adj_hbm,
    first_hbm, pair_hbm, own_hbm, last_hbm, token_ref,
    dest, src, grad, adj, acc, first, pair, sems, adj_sems,
):
    slots = adj.shape[0]
    quarter = grad.shape[2] // BLOCK
    nblocks = grad.shape[0] * quarter
    spread = (acc.shape[0] - 1) // nblocks
    copies = started(
        [(dest_hbm, dest), (src_hbm, src), (grad_hbm, grad)], sems
    )
    spans = [pl.ds(begin, CHUNK) for begin in range(0, slots, CHUNK)]
    adj_copies = started([(adj_hbm.at[span], adj.at[span]) for span in spans], adj_sems)
    acc[...] = jnp.zeros_like(acc)
    core = lax.axis_index("c")
    count = count_ref[0]
    for copy in copies:
        copy.wait()
    for index, copy in enumerate(adj_copies):
        copy.wait()
        products = []
        for j in range(index * CHUNK, (index + 1) * CHUNK):
            target = dest[0, j]
            lane = pl.multiple_of((target % quarter) * BLOCK, BLOCK)
            picked = grad[target // quarter, :, pl.ds(lane, BLOCK)]
            products.append(jnp.dot(picked, adj[j], preferred_element_type=F32))
        for j, product in zip(range(index * CHUNK, (index + 1) * CHUNK), products):
            offset, block = mirrored(src[0, j], core, nblocks, spread)
            place = jnp.where(j < count, offset * nblocks + block, spread * nblocks)
            acc[place] += product
    outs = started(
        [
            (acc.at[pl.ds(2 * nblocks, nblocks)], own_hbm),
            (acc.at[pl.ds(4 * nblocks, nblocks)], last_hbm),
        ],
        sems,
    )
    pair[0] = acc[nblocks : 2 * nblocks].astype(BF16)
    pair[1] = acc[3 * nblocks : 4 * nblocks].astype(BF16)
    outs.append(pltpu.make_async_copy(pair, pair_hbm, sems.at[3]))
    outs[-1].start()
    first[...] = acc[0:nblocks].astype(BF16)
    outs.append(pltpu.make_async_copy(first, first_hbm, sems.at[4]))
    outs[-1].start()
    token_ref[...] = jnp.zeros_like(token_ref)
    for copy in outs:
        copy.wait()


def on_device(
    features, node_order, adj_values, blk_dest, blk_src, blk_count, weight, bias, cotangent
):
    feat, nodes = features.shape
    slots = adj_values.shape[0]
    nblocks = nodes // BLOCK
    parts = lax.axis_size("x")
    out_feat, width = cotangent.shape
    shards = lax.axis_size(ROWS)
    ys, zs = lax.axis_size("y"), lax.axis_size("z")
    scale = 1.0 / math.sqrt(nodes * shards)

    def chip_step(value, sign):
        pairs = [(s, (s + (2 * sign if s % 2 == 0 else -2 * sign)) % shards) for s in range(shards)]
        return lax.ppermute(value, ROWS, pairs)

    def sibling(value):
        return lax.ppermute(value, "c", [(0, 1), (1, 0)])

    slab = jax.ShapeDtypeStruct((feat, nodes), BF16)
    dma = pltpu.SemaphoreType.DMA

    permuted, adj = pl.pallas_call(
        into_order,
        out_shape=(slab, jax.ShapeDtypeStruct(adj_values.shape, BF16)),
        in_specs=[HBM] * 3,
        out_specs=(VMEM, VMEM),
        scratch_shapes=[
            pltpu.VMEM((1, nodes), jnp.int32),
            pltpu.VMEM((feat, nodes), BF16),
            dma((3,)),
        ],
        compiler_params=PARAMS,
        cost_estimate=cost(10**9, 2**20),
        name="into_order",
    )(*in_hbm(node_order, features, adj_values))

    after = chip_step(permuted, -1)
    before = chip_step(permuted, 1)
    beside = sibling(permuted)
    across = sibling(after)

    hidden = pl.pallas_call(
        aggregate,
        out_shape=jax.ShapeDtypeStruct((parts, feat, width), BF16),
        in_specs=[SMEM] + [HBM] * 2 + [VMEM] * 6,
        out_specs=VMEM,
        scratch_shapes=[
            pltpu.SMEM((1, slots), jnp.int32),
            pltpu.SMEM((1, slots), jnp.int32),
            pltpu.VMEM((5 * nblocks, feat, BLOCK), BF16),
            pltpu.VMEM((nblocks + 1, feat, BLOCK), F32),
            dma((2,)),
        ],
        compiler_params=PARAMS,
        cost_estimate=cost(4 * 10**9, 2**22),
        name="aggregate",
    )(blk_count, *in_hbm(blk_dest, blk_src), before, across, permuted, beside, after, adj)

    hidden_rows = lax.all_to_all(hidden, "x", 0, 0).reshape(parts * feat, width)

    output, send = pl.pallas_call(
        dense,
        out_shape=(
            jax.ShapeDtypeStruct((out_feat, width), BF16),
            jax.ShapeDtypeStruct((parts, 2 * feat + 16, width), BF16),
        ),
        in_specs=[VMEM] + [HBM] * 3,
        out_specs=(VMEM, VMEM),
        scratch_shapes=[
            pltpu.VMEM(weight.shape, BF16),
            pltpu.VMEM((1, out_feat), F32),
            pltpu.VMEM((out_feat, width), BF16),
            dma((3,)),
        ],
        compiler_params=PARAMS,
        cost_estimate=cost(10**9, 2**20),
        name="dense",
    )(hidden_rows, *in_hbm(weight, bias[None, :], cotangent))

    recv = lax.all_to_all(send, "x", 0, 0)

    partial, grads = pl.pallas_call(
        first_sum,
        out_shape=(
            pltpu.HBM((2 * ys, 16, BLOCK), F32),
            pltpu.HBM((parts, feat, width), BF16),
        ),
        in_specs=[VMEM],
        out_specs=(HBM, HBM),
        scratch_shapes=[pltpu.VMEM((2 * ys, 16, BLOCK), F32), dma((2,))],
        compiler_params=PARAMS,
        cost_estimate=cost(10**9, 2**20),
        name="first_sum",
    )(recv)
    partial = lax.all_to_all(partial, ("y", "c"), 0, 0)

    first, pair, own, last, token = pl.pallas_call(
        spread_back,
        out_shape=(
            pltpu.HBM((nblocks, feat, BLOCK), BF16),
            pltpu.HBM((2, nblocks, feat, BLOCK), BF16),
            pltpu.HBM((nblocks, feat, BLOCK), F32),
            pltpu.HBM((nblocks, feat, BLOCK), F32),
            jax.ShapeDtypeStruct((8, BLOCK), F32),
        ),
        in_specs=[SMEM] + [HBM] * 4,
        out_specs=(HBM,) * 4 + (VMEM,),
        scratch_shapes=[
            pltpu.SMEM((1, slots), jnp.int32),
            pltpu.SMEM((1, slots), jnp.int32),
            pltpu.VMEM((parts, feat, width), BF16),
            pltpu.VMEM((slots, BLOCK, BLOCK), BF16),
            pltpu.VMEM((5 * nblocks + 1, feat, BLOCK), F32),
            pltpu.VMEM((nblocks, feat, BLOCK), BF16),
            pltpu.VMEM((2, nblocks, feat, BLOCK), BF16),
            dma((5,)),
            dma((slots // CHUNK,)),
        ],
        compiler_params=PARAMS,
        cost_estimate=cost(4 * 10**9, 2**22),
        name="spread_back",
    )(blk_count, *in_hbm(blk_dest, blk_src, grads, adj_values))

    partial, first = pl.pallas_call(
        sum_to_all,
        out_shape=(pltpu.HBM((zs, 16, BLOCK), F32), pltpu.HBM(first.shape, BF16)),
        in_specs=[VMEM, HBM, ANY],
        out_specs=(HBM, HBM),
        scratch_shapes=[pltpu.VMEM((zs, 16, BLOCK), F32), dma((1,))],
        input_output_aliases={1: 1},
        compiler_params=PARAMS,
        cost_estimate=cost(3 * 10**10, 2**20),
        name="sum_to_all",
    )(partial, *in_hbm(first), token)
    partial = lax.all_to_all(partial, "z", 0, 0)

    pair = sibling(pair)
    from_first = chip_step(first, -1)
    last = (last + pair[0].astype(F32)).astype(BF16)
    from_last = chip_step(last, 1)

    pieces, own, grad_b = pl.pallas_call(
        functools.partial(last_sum, scale),
        out_shape=(
            pltpu.HBM((2 * ys, 8, BLOCK), F32),
            pltpu.HBM(own.shape, F32),
            jax.ShapeDtypeStruct((1, out_feat), F32),
        ),
        in_specs=[VMEM, HBM, ANY],
        out_specs=(HBM, HBM, VMEM),
        scratch_shapes=[pltpu.VMEM((2 * ys, 8, BLOCK), F32), dma((1,))],
        input_output_aliases={1: 1},
        compiler_params=PARAMS,
        name="last_sum",
    )(partial, *in_hbm(own), last)
    pieces = lax.all_to_all(pieces, ("y", "c"), 0, 0)

    grad_x, token = pl.pallas_call(
        out_of_order,
        out_shape=(slab, jax.ShapeDtypeStruct((8, BLOCK), F32)),
        in_specs=[HBM] * 2 + [ANY] * 3,
        out_specs=(VMEM, VMEM),
        scratch_shapes=[
            pltpu.VMEM((1, nodes), jnp.int32),
            pltpu.VMEM((nblocks, feat, BLOCK), F32),
            pltpu.VMEM((nblocks, feat, BLOCK), BF16),
            pltpu.VMEM((nblocks, feat, BLOCK), BF16),
            pltpu.VMEM((nblocks, feat, BLOCK), BF16),
            pltpu.VMEM((feat, nodes), BF16),
            dma((5,)),
        ],
        compiler_params=PARAMS,
        cost_estimate=cost(3 * 10**9, 2**21),
        name="out_of_order",
    )(*in_hbm(node_order, own), from_first, pair, from_last)

    whole = pl.pallas_call(
        put_together,
        out_shape=pltpu.HBM((parts, 8 * ys, 2 * BLOCK), F32),
        in_specs=[VMEM, ANY],
        out_specs=HBM,
        scratch_shapes=[pltpu.VMEM((8 * ys, 2 * BLOCK), F32), dma((parts,))],
        compiler_params=PARAMS,
        name="put_together",
    )(pieces, token)
    grad_w = lax.all_to_all(whole, "x", 0, 0).reshape(parts * 8 * ys, 2 * BLOCK)
    return output, grad_x, grad_w, grad_b.reshape(out_feat)


def solution(mesh):
    rows, cols = mesh.devices.shape
    ys = 8 if rows % 16 == 0 else 2
    devices = mesh.devices.reshape(rows // (2 * ys), ys, 2, cols)
    own = Mesh(devices, ("z", "y", "c", "x"))
    in_specs = (
        P("x", ROWS),
        P(ROWS, None),
        P(ROWS, None, None),
        P(ROWS, None),
        P(ROWS, None),
        P(ROWS),
        P(),
        P(),
        P(None, ROWS + ("x",)),
    )
    out_specs = (P(None, ROWS + ("x",)), P("x", ROWS), P(), P())
    return jax.shard_map(
        on_device, mesh=own, in_specs=in_specs, out_specs=out_specs, check_vma=False
    )
```

```python
import functools
import math

import jax
import jax.numpy as jnp
from jax import lax
from jax.experimental import pallas as pl
from jax.experimental.pallas import tpu as pltpu
from jax.sharding import Mesh, PartitionSpec as P

BF16 = jnp.bfloat16
F32 = jnp.float32
BLOCK = 128
TILE = 256
ROWS = ("z", "y", "c")
CHUNK = 8
SPAN = 48
VMEM = pl.BlockSpec(memory_space=pltpu.VMEM)
SMEM = pl.BlockSpec(memory_space=pltpu.SMEM)
HBM = pl.BlockSpec(memory_space=pltpu.HBM)
ANY = pl.BlockSpec(memory_space=pl.ANY)
PARAMS = pltpu.CompilerParams(vmem_limit_bytes=40 * 1024 * 1024)


def in_hbm(*arrays):
    return tuple(pltpu.with_memory_space_constraint(array, pltpu.HBM) for array in arrays)


def in_smem(*arrays):
    return tuple(pltpu.with_memory_space_constraint(array, pltpu.SMEM) for array in arrays)


def cost(flops, size):
    return pl.CostEstimate(flops=flops, bytes_accessed=size, transcendentals=0)


def started(pairs, sems):
    copies = [pltpu.make_async_copy(a, b, sems.at[i]) for i, (a, b) in enumerate(pairs)]
    for copy in copies:
        copy.start()
    return copies


def split(index, size):
    return index >> (size.bit_length() - 1), index & (size - 1)


def into_order(order_hbm, x_hbm, adj_hbm, out_ref, adj_ref, order, x, sems):
    copies = started([(x_hbm, x), (order_hbm, order), (adj_hbm, adj_ref)], sems)
    copies[0].wait()
    copies[1].wait()
    count = x.shape[1]
    for start in range(0, count, TILE):
        group, lane = split(order[:, start : start + TILE], BLOCK)
        rows = lax.broadcasted_iota(jnp.int32, (BLOCK, TILE), 0)
        hot = jnp.where(lane == rows, 1.0, 0.0).astype(BF16)
        moved = jnp.zeros((x.shape[0], TILE), F32)
        for g in range(count // BLOCK):
            part = jnp.dot(x[:, g * BLOCK : (g + 1) * BLOCK], hot, preferred_element_type=F32)
            moved = jnp.where(group == g, part, moved)
        out_ref[:, start : start + TILE] = moved.astype(BF16)
    copies[2].wait()


def out_of_order(
    order_hbm, own_hbm, first_hbm, pair_hbm, last_hbm, out_ref, token_ref, order, own, first, near, last, total, sems
):
    copies = started(
        [
            (last_hbm, last),
            (first_hbm, first),
            (pair_hbm.at[1], near),
            (own_hbm, own),
            (order_hbm, order),
        ],
        sems,
    )
    token_ref[...] = jnp.zeros_like(token_ref)
    for copy in copies:
        copy.wait()
    for block in range(own.shape[0]):
        sums = own[block] + near[block].astype(F32)
        sums = sums + first[block].astype(F32) + last[block].astype(F32)
        total[:, block * BLOCK : (block + 1) * BLOCK] = sums.astype(BF16)
    count = total.shape[1]
    for start in range(0, count, TILE):
        rows = lax.broadcasted_iota(jnp.int32, (TILE, count), 0) + start
        hot = jnp.where(order[...] == rows, 1.0, 0.0).astype(BF16)
        moved = lax.dot_general(
            total[...], hot, (((1,), (1,)), ((), ())), preferred_element_type=F32
        )
        out_ref[:, start : start + TILE] = moved.astype(BF16)


def sum_to_all(recv, first_hbm, token, out_hbm, kept_hbm, out, sems):
    total = jnp.sum(recv[...], axis=0)
    for i in range(out.shape[0]):
        out[i] = total
    started([(out, out_hbm)], sems)[0].wait()


def last_sum(scale, recv, own_hbm, token, out_hbm, kept_hbm, bias_ref, out, sems):
    total = jnp.sum(recv[...], axis=0) * scale
    for i in range(out.shape[0]):
        out[i] = total[0:8]
    copies = started([(out, out_hbm)], sems)
    bias_ref[:, 0:BLOCK] = total[8:9]
    bias_ref[:, BLOCK:] = total[12:13]
    copies[0].wait()


def put_together(parts, recv, token, out_ref):
    rows = out_ref.shape[0] // parts
    for i in range(recv.shape[0]):
        y, c, x = i // (2 * parts), i // parts % 2, i % parts
        row, lane = x * rows + 8 * y, c * BLOCK
        out_ref[row : row + 8, lane : lane + BLOCK] = recv[i]


def mirrored(source, core, nblocks, spread):
    offset, block = split(source, nblocks)
    return jnp.where(core == 0, offset, spread - 1 - offset) * nblocks + block


def turned(adj, out_ref):
    for j in range(adj.shape[0]):
        out_ref[j] = adj[j].T


def aggregate(
    count_ref, dest, src, before, across, permuted, beside, after, adj, out_ref, win, acc
):
    slots = adj.shape[0]
    nblocks = acc.shape[0] - 1
    spread = win.shape[0] // nblocks
    quarter = out_ref.shape[2] // BLOCK
    acc[...] = jnp.zeros_like(acc)
    for block in range(nblocks):
        lane = slice(block * BLOCK, (block + 1) * BLOCK)
        win[block] = before[:, lane]
        win[nblocks + block] = across[:, lane]
        win[2 * nblocks + block] = permuted[:, lane]
        win[3 * nblocks + block] = beside[:, lane]
        win[4 * nblocks + block] = after[:, lane]
    core = lax.axis_index("c")
    count = count_ref[0]
    for begin in range(0, slots, CHUNK):
        products = []
        for j in range(begin, begin + CHUNK):
            place = mirrored(src[0, j], core, nblocks, spread)
            products.append(
                jnp.dot(win[place], adj[j], preferred_element_type=F32)
            )
        for j, product in zip(range(begin, begin + CHUNK), products):
            target = jnp.where(j < count, dest[0, j], nblocks)
            acc[target] += product
    for block in range(nblocks):
        lane = (block % quarter) * BLOCK
        out_ref[block // quarter, :, lane : lane + BLOCK] = acc[block].astype(BF16)


def dense(hidden_ref, weight_hbm, bias_hbm, cot_hbm, out_ref, send_ref, weight_v, bias_v, cot, sems):
    copies = started([(weight_hbm, weight_v), (bias_hbm, bias_v), (cot_hbm, cot)], sems)
    feat, width = hidden_ref.shape
    part = send_ref.shape[0]
    rows = feat // part
    hidden = hidden_ref[...]
    copies[0].wait()
    copies[1].wait()
    weight = weight_v[...]
    bias = jnp.broadcast_to(bias_v[...], (BLOCK, bias_v.shape[1])).T
    bias = jnp.concatenate([bias] * (width // BLOCK), axis=1)
    v = (
        lax.dot_general(weight, hidden, (((0,), (0,)), ((), ())), preferred_element_type=F32)
        + bias
    )
    root = math.sqrt(2.0 / math.pi)
    square = v * v
    t = jnp.tanh(root * (v + 0.044715 * (square * v)))
    half = 0.5 * (1.0 + t)
    out_ref[...] = (v * half).astype(BF16)
    slope = half + (0.5 * root) * v * (1.0 - t * t) * (1.0 + (3.0 * 0.044715) * square)
    copies[2].wait()
    grad = (cot[...].astype(F32) * slope).astype(BF16)
    back = jnp.dot(weight, grad, preferred_element_type=F32).astype(BF16)
    grad_w = lax.dot_general(hidden, grad, (((1,), (1,)), ((), ())), preferred_element_type=F32)
    ones = jnp.ones((16, width), BF16)
    grad_b = lax.dot_general(ones, grad, (((1,), (1,)), ((), ())), preferred_element_type=F32)
    high_w = grad_w.astype(BF16)
    low_w = (grad_w - high_w.astype(F32)).astype(BF16)
    high_b = grad_b.astype(BF16)
    low_b = (grad_b - high_b.astype(F32)).astype(BF16)
    half_width = grad_w.shape[1]
    for i in range(part):
        span = slice(i * rows, (i + 1) * rows)
        send_ref[i, 0:rows, :] = back[span]
        send_ref[i, rows : 2 * rows, 0:half_width] = high_w[span]
        send_ref[i, rows : 2 * rows, half_width:] = low_w[span]
        send_ref[i, 2 * rows :, 0:half_width] = high_b
        send_ref[i, 2 * rows :, half_width:] = low_b


def first_sum(recv, out_hbm, grad_hbm, out, sems):
    rows = grad_hbm.shape[1]
    half_width = recv.shape[2] // 2
    copies = started([(recv.at[:, pl.ds(0, rows), :], grad_hbm)], sems)
    total = jnp.zeros((rows + 16, half_width), F32)
    for i in range(recv.shape[0]):
        total = total + recv[i, rows:, 0:half_width].astype(F32)
        total = total + recv[i, rows:, half_width:].astype(F32)
    for i in range(out.shape[0] // 2):
        for c in range(2):
            lane = slice(c * BLOCK, (c + 1) * BLOCK)
            out[2 * i + c, 0:8, :] = total[8 * i : 8 * i + 8, lane]
            out[2 * i + c, 8:12, :] = total[rows : rows + 4, 0:BLOCK]
            out[2 * i + c, 12:16, :] = total[rows : rows + 4, BLOCK : 2 * BLOCK]
    last = pltpu.make_async_copy(out, out_hbm, sems.at[1])
    last.start()
    copies[0].wait()
    last.wait()


def spread_back(
    count_ref, dest_hbm, src_hbm, grad_hbm, adj_hbm,
    first_hbm, pair_hbm, own_hbm, last_hbm, token_ref,
    dest, src, grad, adj, acc, first, pair, sems, adj_sems,
):
    slots = adj.shape[0]
    quarter = grad.shape[2] // BLOCK
    nblocks = grad.shape[0] * quarter
    spread = (acc.shape[0] - 1) // nblocks
    copies = started(
        [(dest_hbm, dest), (src_hbm, src), (grad_hbm, grad)], sems
    )
    spans = [pl.ds(begin, SPAN) for begin in range(0, slots, SPAN)]
    adj_copies = started([(adj_hbm.at[span], adj.at[span]) for span in spans], adj_sems)
    acc[...] = jnp.zeros_like(acc)
    core = lax.axis_index("c")
    count = count_ref[0]
    for copy in copies:
        copy.wait()
    for index, copy in enumerate(adj_copies):
        copy.wait()
        products = []
        for j in range(index * SPAN, (index + 1) * SPAN):
            part, place = split(dest[0, j], quarter)
            picked = grad[part, :, pl.ds(pl.multiple_of(place * BLOCK, BLOCK), BLOCK)]
            products.append(jnp.dot(picked, adj[j], preferred_element_type=F32))
        for j, product in zip(range(index * SPAN, (index + 1) * SPAN), products):
            place = mirrored(src[0, j], core, nblocks, spread)
            place = jnp.where(j < count, place, spread * nblocks)
            acc[place] += product
    outs = started(
        [
            (acc.at[pl.ds(2 * nblocks, nblocks)], own_hbm),
            (acc.at[pl.ds(4 * nblocks, nblocks)], last_hbm),
        ],
        sems,
    )
    pair[0] = acc[nblocks : 2 * nblocks].astype(BF16)
    pair[1] = acc[3 * nblocks : 4 * nblocks].astype(BF16)
    outs.append(pltpu.make_async_copy(pair, pair_hbm, sems.at[3]))
    outs[-1].start()
    first[...] = acc[0:nblocks].astype(BF16)
    outs.append(pltpu.make_async_copy(first, first_hbm, sems.at[4]))
    outs[-1].start()
    token_ref[...] = jnp.zeros_like(token_ref)
    for copy in outs:
        copy.wait()


def on_device(
    features, node_order, adj_values, blk_dest, blk_src, blk_count, weight, bias, cotangent
):
    feat, nodes = features.shape
    slots = adj_values.shape[0]
    nblocks = nodes // BLOCK
    parts = lax.axis_size("x")
    out_feat, width = cotangent.shape
    shards = lax.axis_size(ROWS)
    ys, zs = lax.axis_size("y"), lax.axis_size("z")
    scale = 1.0 / math.sqrt(nodes * shards)

    def chip_step(value, sign):
        pairs = [(s, (s + (2 * sign if s % 2 == 0 else -2 * sign)) % shards) for s in range(shards)]
        return lax.ppermute(value, ROWS, pairs)

    def sibling(value):
        return lax.ppermute(value, "c", [(0, 1), (1, 0)])

    slab = jax.ShapeDtypeStruct((feat, nodes), BF16)
    dma = pltpu.SemaphoreType.DMA

    permuted, adj = pl.pallas_call(
        into_order,
        out_shape=(slab, jax.ShapeDtypeStruct(adj_values.shape, BF16)),
        in_specs=[HBM] * 3,
        out_specs=(VMEM, VMEM),
        scratch_shapes=[
            pltpu.VMEM((1, nodes), jnp.int32),
            pltpu.VMEM((feat, nodes), BF16),
            dma((3,)),
        ],
        compiler_params=PARAMS,
        cost_estimate=cost(10**9, 2**20),
        name="into_order",
    )(*in_hbm(node_order, features, adj_values))

    across_adj = pl.pallas_call(
        turned,
        out_shape=jax.ShapeDtypeStruct(adj_values.shape, BF16),
        in_specs=[VMEM],
        out_specs=VMEM,
        compiler_params=PARAMS,
        cost_estimate=cost(2 * 10**9, 2**20),
        name="turned",
    )(adj)
    after = chip_step(permuted, -1)
    before = chip_step(permuted, 1)
    beside = sibling(permuted)
    across = sibling(after)

    hidden = pl.pallas_call(
        aggregate,
        out_shape=jax.ShapeDtypeStruct((parts, feat, width), BF16),
        in_specs=[SMEM] * 3 + [VMEM] * 6,
        out_specs=VMEM,
        scratch_shapes=[
            pltpu.VMEM((5 * nblocks, feat, BLOCK), BF16),
            pltpu.VMEM((nblocks + 1, feat, BLOCK), F32),
        ],
        compiler_params=PARAMS,
        cost_estimate=cost(4 * 10**9, 2**22),
        name="aggregate",
    )(blk_count, *in_smem(blk_dest, blk_src), before, across, permuted, beside, after, across_adj)

    hidden_rows = lax.all_to_all(hidden, "x", 0, 0).reshape(parts * feat, width)

    output, send = pl.pallas_call(
        dense,
        out_shape=(
            jax.ShapeDtypeStruct((out_feat, width), BF16),
            jax.ShapeDtypeStruct((parts, 2 * feat + 16, width), BF16),
        ),
        in_specs=[VMEM] + [HBM] * 3,
        out_specs=(VMEM, VMEM),
        scratch_shapes=[
            pltpu.VMEM(weight.shape, BF16),
            pltpu.VMEM((1, out_feat), F32),
            pltpu.VMEM((out_feat, width), BF16),
            dma((3,)),
        ],
        compiler_params=PARAMS,
        cost_estimate=cost(10**9, 2**20),
        name="dense",
    )(hidden_rows, *in_hbm(weight, bias[None, :], cotangent))

    recv = lax.all_to_all(send, "x", 0, 0)

    partial, grads = pl.pallas_call(
        first_sum,
        out_shape=(
            pltpu.HBM((2 * ys, 16, BLOCK), F32),
            pltpu.HBM((parts, feat, width), BF16),
        ),
        in_specs=[VMEM],
        out_specs=(HBM, HBM),
        scratch_shapes=[pltpu.VMEM((2 * ys, 16, BLOCK), F32), dma((2,))],
        compiler_params=PARAMS,
        cost_estimate=cost(10**9, 2**20),
        name="first_sum",
    )(recv)
    partial = lax.all_to_all(partial, ("y", "c"), 0, 0)

    first, pair, own, last, token = pl.pallas_call(
        spread_back,
        out_shape=(
            pltpu.HBM((nblocks, feat, BLOCK), BF16),
            pltpu.HBM((2, nblocks, feat, BLOCK), BF16),
            pltpu.HBM((nblocks, feat, BLOCK), F32),
            pltpu.HBM((nblocks, feat, BLOCK), F32),
            jax.ShapeDtypeStruct((8, BLOCK), F32),
        ),
        in_specs=[SMEM] + [HBM] * 4,
        out_specs=(HBM,) * 4 + (VMEM,),
        scratch_shapes=[
            pltpu.SMEM((1, slots), jnp.int32),
            pltpu.SMEM((1, slots), jnp.int32),
            pltpu.VMEM((parts, feat, width), BF16),
            pltpu.VMEM((slots, BLOCK, BLOCK), BF16),
            pltpu.VMEM((5 * nblocks + 1, feat, BLOCK), F32),
            pltpu.VMEM((nblocks, feat, BLOCK), BF16),
            pltpu.VMEM((2, nblocks, feat, BLOCK), BF16),
            dma((5,)),
            dma((slots // SPAN,)),
        ],
        compiler_params=PARAMS,
        cost_estimate=cost(4 * 10**9, 2**22),
        name="spread_back",
    )(blk_count, *in_hbm(blk_dest, blk_src, grads, adj_values))

    partial, first = pl.pallas_call(
        sum_to_all,
        out_shape=(pltpu.HBM((zs, 16, BLOCK), F32), pltpu.HBM(first.shape, BF16)),
        in_specs=[VMEM, HBM, ANY],
        out_specs=(HBM, HBM),
        scratch_shapes=[pltpu.VMEM((zs, 16, BLOCK), F32), dma((1,))],
        input_output_aliases={1: 1},
        compiler_params=PARAMS,
        cost_estimate=cost(3 * 10**10, 2**20),
        name="sum_to_all",
    )(partial, *in_hbm(first), token)
    partial = lax.all_to_all(partial, "z", 0, 0)

    pair = sibling(pair)
    from_first = chip_step(first, -1)
    last = (last + pair[0].astype(F32)).astype(BF16)
    from_last = chip_step(last, 1)

    pieces, own, grad_b = pl.pallas_call(
        functools.partial(last_sum, scale),
        out_shape=(
            pltpu.HBM((2 * ys * parts, 8, BLOCK), F32),
            pltpu.HBM(own.shape, F32),
            jax.ShapeDtypeStruct((1, out_feat), F32),
        ),
        in_specs=[VMEM, HBM, ANY],
        out_specs=(HBM, HBM, VMEM),
        scratch_shapes=[pltpu.VMEM((2 * ys * parts, 8, BLOCK), F32), dma((1,))],
        input_output_aliases={1: 1},
        compiler_params=PARAMS,
        name="last_sum",
    )(partial, *in_hbm(own), last)
    pieces = lax.all_to_all(pieces, ("y", "c", "x"), 0, 0)

    grad_x, token = pl.pallas_call(
        out_of_order,
        out_shape=(slab, jax.ShapeDtypeStruct((8, BLOCK), F32)),
        in_specs=[HBM] * 2 + [ANY] * 3,
        out_specs=(VMEM, VMEM),
        scratch_shapes=[
            pltpu.VMEM((1, nodes), jnp.int32),
            pltpu.VMEM((nblocks, feat, BLOCK), F32),
            pltpu.VMEM((nblocks, feat, BLOCK), BF16),
            pltpu.VMEM((nblocks, feat, BLOCK), BF16),
            pltpu.VMEM((nblocks, feat, BLOCK), BF16),
            pltpu.VMEM((feat, nodes), BF16),
            dma((5,)),
        ],
        compiler_params=PARAMS,
        cost_estimate=cost(3 * 10**9, 2**21),
        name="out_of_order",
    )(*in_hbm(node_order, own), from_first, pair, from_last)

    grad_w = pl.pallas_call(
        functools.partial(put_together, parts),
        out_shape=jax.ShapeDtypeStruct((parts * 8 * ys, 2 * BLOCK), F32),
        in_specs=[VMEM, ANY],
        out_specs=VMEM,
        compiler_params=PARAMS,
        name="put_together",
    )(pieces, token)
    return output, grad_x, grad_w, grad_b.reshape(out_feat)


def solution(mesh):
    rows, cols = mesh.devices.shape
    ys = 8 if rows % 16 == 0 else 2
    devices = mesh.devices.reshape(rows // (2 * ys), ys, 2, cols)
    own = Mesh(devices, ("z", "y", "c", "x"))
    in_specs = (
        P("x", ROWS),
        P(ROWS, None),
        P(ROWS, None, None),
        P(ROWS, None),
        P(ROWS, None),
        P(ROWS),
        P(),
        P(),
        P(None, ROWS + ("x",)),
    )
    out_specs = (P(None, ROWS + ("x",)), P("x", ROWS), P(), P())
    return jax.shard_map(
        on_device, mesh=own, in_specs=in_specs, out_specs=out_specs, check_vma=False
    )
```

```python
import functools
import math

import jax
import jax.numpy as jnp
from jax import lax
from jax.experimental import pallas as pl
from jax.experimental.pallas import tpu as pltpu
from jax.sharding import Mesh, PartitionSpec as P

BF16 = jnp.bfloat16
F32 = jnp.float32
BLOCK = 128
TILE = 256
ROWS = ("z", "y", "c")
CHUNK = 8
SPAN = 48
VMEM = pl.BlockSpec(memory_space=pltpu.VMEM)
SMEM = pl.BlockSpec(memory_space=pltpu.SMEM)
HBM = pl.BlockSpec(memory_space=pltpu.HBM)
ANY = pl.BlockSpec(memory_space=pl.ANY)
PARAMS = pltpu.CompilerParams(vmem_limit_bytes=40 * 1024 * 1024)


def in_hbm(*arrays):
    return tuple(pltpu.with_memory_space_constraint(array, pltpu.HBM) for array in arrays)


def in_smem(*arrays):
    return tuple(pltpu.with_memory_space_constraint(array, pltpu.SMEM) for array in arrays)


def cost(flops, size):
    return pl.CostEstimate(flops=flops, bytes_accessed=size, transcendentals=0)


def started(pairs, sems):
    copies = [pltpu.make_async_copy(a, b, sems.at[i]) for i, (a, b) in enumerate(pairs)]
    for copy in copies:
        copy.start()
    return copies


def split(index, size):
    return index >> (size.bit_length() - 1), index & (size - 1)


def into_order(order_hbm, x_hbm, adj_hbm, out_ref, adj_ref, order, x, sems):
    copies = started([(x_hbm, x), (order_hbm, order), (adj_hbm, adj_ref)], sems)
    copies[0].wait()
    copies[1].wait()
    count = x.shape[1]
    for start in range(0, count, TILE):
        group, lane = split(order[:, start : start + TILE], BLOCK)
        rows = lax.broadcasted_iota(jnp.int32, (BLOCK, TILE), 0)
        hot = jnp.where(lane == rows, 1.0, 0.0).astype(BF16)
        moved = jnp.zeros((x.shape[0], TILE), F32)
        for g in range(count // BLOCK):
            part = jnp.dot(x[:, g * BLOCK : (g + 1) * BLOCK], hot, preferred_element_type=F32)
            moved = jnp.where(group == g, part, moved)
        out_ref[:, start : start + TILE] = moved.astype(BF16)
    copies[2].wait()


def out_of_order(
    order_hbm, own_hbm, first_hbm, pair_hbm, last_hbm, out_ref, token_ref, order, own, first, near, last, total, sems
):
    copies = started(
        [
            (last_hbm, last),
            (first_hbm, first),
            (pair_hbm.at[1], near),
            (own_hbm, own),
            (order_hbm, order),
        ],
        sems,
    )
    token_ref[...] = jnp.zeros_like(token_ref)
    for copy in copies:
        copy.wait()
    for block in range(own.shape[0]):
        sums = own[block] + near[block].astype(F32)
        sums = sums + first[block].astype(F32) + last[block].astype(F32)
        total[:, block * BLOCK : (block + 1) * BLOCK] = sums.astype(BF16)
    count = total.shape[1]
    for start in range(0, count, TILE):
        rows = lax.broadcasted_iota(jnp.int32, (TILE, count), 0) + start
        hot = jnp.where(order[...] == rows, 1.0, 0.0).astype(BF16)
        moved = lax.dot_general(
            total[...], hot, (((1,), (1,)), ((), ())), preferred_element_type=F32
        )
        out_ref[:, start : start + TILE] = moved.astype(BF16)


def sum_to_all(recv, token, out_hbm, out, sems):
    total = jnp.sum(recv[...], axis=0)
    for i in range(out.shape[0]):
        out[i] = total
    started([(out, out_hbm)], sems)[0].wait()


def last_sum(scale, recv, own_hbm, token, returned, out_hbm, kept_hbm, bias_ref, out, sems):
    total = jnp.sum(recv[...], axis=0) * scale
    for i in range(out.shape[0]):
        out[i] = total[0:8]
    copies = started([(out, out_hbm)], sems)
    bias_ref[:, 0:BLOCK] = total[8:9]
    bias_ref[:, BLOCK:] = total[12:13]
    copies[0].wait()


def put_together(parts, recv, token, out_ref):
    rows = out_ref.shape[0] // parts
    for i in range(recv.shape[0]):
        y, c, x = i // (2 * parts), i // parts % 2, i % parts
        row, lane = x * rows + 8 * y, c * BLOCK
        out_ref[row : row + 8, lane : lane + BLOCK] = recv[i]


def mirrored(source, core, nblocks, spread):
    offset, block = split(source, nblocks)
    return jnp.where(core == 0, offset, spread - 1 - offset) * nblocks + block


def turned(adj, out_ref):
    for j in range(adj.shape[0]):
        out_ref[j] = adj[j].T


def aggregate(
    count_ref, dest, src, beside, across, permuted, before, after, adj, out_ref, win, acc
):
    slots = adj.shape[0]
    nblocks = acc.shape[0] - 1
    spread = win.shape[0] // nblocks
    quarter = out_ref.shape[2] // BLOCK
    acc[...] = jnp.zeros_like(acc)
    for block in range(nblocks):
        lane = slice(block * BLOCK, (block + 1) * BLOCK)
        win[block] = before[:, lane]
        win[nblocks + block] = across[:, lane]
        win[2 * nblocks + block] = permuted[:, lane]
        win[3 * nblocks + block] = beside[:, lane]
        win[4 * nblocks + block] = after[:, lane]
    core = lax.axis_index("c")
    count = count_ref[0]
    for begin in range(0, slots, CHUNK):
        products = []
        for j in range(begin, begin + CHUNK):
            place = mirrored(src[0, j], core, nblocks, spread)
            products.append(
                jnp.dot(win[place], adj[j], preferred_element_type=F32)
            )
        for j, product in zip(range(begin, begin + CHUNK), products):
            target = jnp.where(j < count, dest[0, j], nblocks)
            acc[target] += product
    for block in range(nblocks):
        lane = (block % quarter) * BLOCK
        out_ref[block // quarter, :, lane : lane + BLOCK] = acc[block].astype(BF16)


def dense(hidden_ref, weight_hbm, bias_hbm, cot_hbm, out_ref, send_ref, weight_v, bias_v, cot, sems):
    copies = started([(weight_hbm, weight_v), (bias_hbm, bias_v), (cot_hbm, cot)], sems)
    feat, width = hidden_ref.shape
    part = send_ref.shape[0]
    rows = feat // part
    hidden = hidden_ref[...]
    copies[0].wait()
    copies[1].wait()
    weight = weight_v[...]
    bias = jnp.broadcast_to(bias_v[...], (BLOCK, bias_v.shape[1])).T
    bias = jnp.concatenate([bias] * (width // BLOCK), axis=1)
    v = (
        lax.dot_general(weight, hidden, (((0,), (0,)), ((), ())), preferred_element_type=F32)
        + bias
    )
    root = math.sqrt(2.0 / math.pi)
    square = v * v
    t = jnp.tanh(root * (v + 0.044715 * (square * v)))
    half = 0.5 * (1.0 + t)
    out_ref[...] = (v * half).astype(BF16)
    slope = half + (0.5 * root) * v * (1.0 - t * t) * (1.0 + (3.0 * 0.044715) * square)
    copies[2].wait()
    grad = (cot[...].astype(F32) * slope).astype(BF16)
    back = jnp.dot(weight, grad, preferred_element_type=F32).astype(BF16)
    grad_w = lax.dot_general(hidden, grad, (((1,), (1,)), ((), ())), preferred_element_type=F32)
    ones = jnp.ones((16, width), BF16)
    grad_b = lax.dot_general(ones, grad, (((1,), (1,)), ((), ())), preferred_element_type=F32)
    high_w = grad_w.astype(BF16)
    low_w = (grad_w - high_w.astype(F32)).astype(BF16)
    high_b = grad_b.astype(BF16)
    low_b = (grad_b - high_b.astype(F32)).astype(BF16)
    half_width = grad_w.shape[1]
    for i in range(part):
        span = slice(i * rows, (i + 1) * rows)
        send_ref[i, 0:rows, :] = back[span]
        send_ref[i, rows : 2 * rows, 0:half_width] = high_w[span]
        send_ref[i, rows : 2 * rows, half_width:] = low_w[span]
        send_ref[i, 2 * rows :, 0:half_width] = high_b
        send_ref[i, 2 * rows :, half_width:] = low_b


def first_sum(recv, out_hbm, grad_hbm, out, sems):
    rows = grad_hbm.shape[1]
    half_width = recv.shape[2] // 2
    copies = started([(recv.at[:, pl.ds(0, rows), :], grad_hbm)], sems)
    total = jnp.zeros((rows + 16, half_width), F32)
    for i in range(recv.shape[0]):
        total = total + recv[i, rows:, 0:half_width].astype(F32)
        total = total + recv[i, rows:, half_width:].astype(F32)
    for i in range(out.shape[0] // 2):
        for c in range(2):
            lane = slice(c * BLOCK, (c + 1) * BLOCK)
            out[2 * i + c, 0:8, :] = total[8 * i : 8 * i + 8, lane]
            out[2 * i + c, 8:12, :] = total[rows : rows + 4, 0:BLOCK]
            out[2 * i + c, 12:16, :] = total[rows : rows + 4, BLOCK : 2 * BLOCK]
    last = pltpu.make_async_copy(out, out_hbm, sems.at[1])
    last.start()
    copies[0].wait()
    last.wait()


def spread_back(
    count_ref, dest_hbm, src_hbm, grad_hbm, adj_hbm,
    first_hbm, pair_hbm, own_hbm, last_hbm, token_ref,
    dest, src, grad, adj, acc, first, pair, sems, adj_sems,
):
    slots = adj.shape[0]
    quarter = grad.shape[2] // BLOCK
    nblocks = grad.shape[0] * quarter
    spread = (acc.shape[0] - 1) // nblocks
    copies = started(
        [(dest_hbm, dest), (src_hbm, src), (grad_hbm, grad)], sems
    )
    spans = [pl.ds(begin, SPAN) for begin in range(0, slots, SPAN)]
    adj_copies = started([(adj_hbm.at[span], adj.at[span]) for span in spans], adj_sems)
    acc[...] = jnp.zeros_like(acc)
    core = lax.axis_index("c")
    count = count_ref[0]
    for copy in copies:
        copy.wait()
    for index, copy in enumerate(adj_copies):
        copy.wait()
        products = []
        for j in range(index * SPAN, (index + 1) * SPAN):
            part, place = split(dest[0, j], quarter)
            picked = grad[part, :, pl.ds(pl.multiple_of(place * BLOCK, BLOCK), BLOCK)]
            products.append(jnp.dot(picked, adj[j], preferred_element_type=F32))
        for j, product in zip(range(index * SPAN, (index + 1) * SPAN), products):
            place = mirrored(src[0, j], core, nblocks, spread)
            place = jnp.where(j < count, place, spread * nblocks)
            acc[place] += product
    outs = started(
        [
            (acc.at[pl.ds(2 * nblocks, nblocks)], own_hbm),
            (acc.at[pl.ds(4 * nblocks, nblocks)], last_hbm),
        ],
        sems,
    )
    pair[0] = acc[nblocks : 2 * nblocks].astype(BF16)
    pair[1] = acc[3 * nblocks : 4 * nblocks].astype(BF16)
    outs.append(pltpu.make_async_copy(pair, pair_hbm, sems.at[3]))
    outs[-1].start()
    first[...] = acc[0:nblocks].astype(BF16)
    outs.append(pltpu.make_async_copy(first, first_hbm, sems.at[4]))
    outs[-1].start()
    token_ref[...] = jnp.zeros_like(token_ref)
    for copy in outs:
        copy.wait()


def on_device(
    features, node_order, adj_values, blk_dest, blk_src, blk_count, weight, bias, cotangent
):
    feat, nodes = features.shape
    slots = adj_values.shape[0]
    nblocks = nodes // BLOCK
    parts = lax.axis_size("x")
    out_feat, width = cotangent.shape
    shards = lax.axis_size(ROWS)
    ys, zs = lax.axis_size("y"), lax.axis_size("z")
    scale = 1.0 / math.sqrt(nodes * shards)

    def chip_step(value, sign):
        pairs = [(s, (s + (2 * sign if s % 2 == 0 else -2 * sign)) % shards) for s in range(shards)]
        return lax.ppermute(value, ROWS, pairs)

    def sibling(value):
        return lax.ppermute(value, "c", [(0, 1), (1, 0)])

    slab = jax.ShapeDtypeStruct((feat, nodes), BF16)
    dma = pltpu.SemaphoreType.DMA

    permuted, adj = pl.pallas_call(
        into_order,
        out_shape=(slab, jax.ShapeDtypeStruct(adj_values.shape, BF16)),
        in_specs=[HBM] * 3,
        out_specs=(VMEM, VMEM),
        scratch_shapes=[
            pltpu.VMEM((1, nodes), jnp.int32),
            pltpu.VMEM((feat, nodes), BF16),
            dma((3,)),
        ],
        compiler_params=PARAMS,
        cost_estimate=cost(10**9, 2**20),
        name="into_order",
    )(*in_hbm(node_order, features, adj_values))

    adj_turned = pl.pallas_call(
        turned,
        out_shape=jax.ShapeDtypeStruct(adj_values.shape, BF16),
        in_specs=[VMEM],
        out_specs=VMEM,
        compiler_params=PARAMS,
        cost_estimate=cost(2 * 10**9, 2**20),
        name="turned",
    )(adj)
    after = chip_step(permuted, -1)
    before = chip_step(permuted, 1)
    beside = sibling(permuted)
    across = sibling(after)

    hidden = pl.pallas_call(
        aggregate,
        out_shape=jax.ShapeDtypeStruct((parts, feat, width), BF16),
        in_specs=[SMEM] * 3 + [VMEM] * 6,
        out_specs=VMEM,
        scratch_shapes=[
            pltpu.VMEM((5 * nblocks, feat, BLOCK), BF16),
            pltpu.VMEM((nblocks + 1, feat, BLOCK), F32),
        ],
        compiler_params=PARAMS,
        cost_estimate=cost(4 * 10**9, 2**22),
        name="aggregate",
    )(blk_count, *in_smem(blk_dest, blk_src), beside, across, permuted, before, after, adj_turned)

    hidden_rows = lax.all_to_all(hidden, "x", 0, 0).reshape(parts * feat, width)

    output, send = pl.pallas_call(
        dense,
        out_shape=(
            jax.ShapeDtypeStruct((out_feat, width), BF16),
            jax.ShapeDtypeStruct((parts, 2 * feat + 16, width), BF16),
        ),
        in_specs=[VMEM] + [HBM] * 3,
        out_specs=(VMEM, VMEM),
        scratch_shapes=[
            pltpu.VMEM(weight.shape, BF16),
            pltpu.VMEM((1, out_feat), F32),
            pltpu.VMEM((out_feat, width), BF16),
            dma((3,)),
        ],
        compiler_params=PARAMS,
        cost_estimate=cost(10**9, 2**20),
        name="dense",
    )(hidden_rows, *in_hbm(weight, bias[None, :], cotangent))

    recv = lax.all_to_all(send, "x", 0, 0)

    partial, grads = pl.pallas_call(
        first_sum,
        out_shape=(
            pltpu.HBM((2 * ys, 16, BLOCK), F32),
            pltpu.HBM((parts, feat, width), BF16),
        ),
        in_specs=[VMEM],
        out_specs=(HBM, HBM),
        scratch_shapes=[pltpu.VMEM((2 * ys, 16, BLOCK), F32), dma((2,))],
        compiler_params=PARAMS,
        cost_estimate=cost(10**9, 2**20),
        name="first_sum",
    )(recv)
    partial = lax.all_to_all(partial, ("y", "c"), 0, 0)

    first, pair, own, last, token = pl.pallas_call(
        spread_back,
        out_shape=(
            pltpu.HBM((nblocks, feat, BLOCK), BF16),
            pltpu.HBM((2, nblocks, feat, BLOCK), BF16),
            pltpu.HBM((nblocks, feat, BLOCK), F32),
            pltpu.HBM((nblocks, feat, BLOCK), F32),
            jax.ShapeDtypeStruct((8, BLOCK), F32),
        ),
        in_specs=[SMEM] + [HBM] * 4,
        out_specs=(HBM,) * 4 + (VMEM,),
        scratch_shapes=[
            pltpu.SMEM((1, slots), jnp.int32),
            pltpu.SMEM((1, slots), jnp.int32),
            pltpu.VMEM((parts, feat, width), BF16),
            pltpu.VMEM((slots, BLOCK, BLOCK), BF16),
            pltpu.VMEM((5 * nblocks + 1, feat, BLOCK), F32),
            pltpu.VMEM((nblocks, feat, BLOCK), BF16),
            pltpu.VMEM((2, nblocks, feat, BLOCK), BF16),
            dma((5,)),
            dma((slots // SPAN,)),
        ],
        compiler_params=PARAMS,
        cost_estimate=cost(4 * 10**9, 2**22),
        name="spread_back",
    )(blk_count, *in_hbm(blk_dest, blk_src, grads, adj_values))

    partial = pl.pallas_call(
        sum_to_all,
        out_shape=pltpu.HBM((zs, 16, BLOCK), F32),
        in_specs=[VMEM, ANY],
        out_specs=HBM,
        scratch_shapes=[pltpu.VMEM((zs, 16, BLOCK), F32), dma((1,))],
        compiler_params=PARAMS,
        cost_estimate=cost(3 * 10**10, 2**20),
        name="sum_to_all",
    )(partial, token)
    partial = lax.all_to_all(partial, "z", 0, 0)

    pair = sibling(pair)
    from_first = chip_step(first, -1)
    last = (last + pair[0].astype(F32)).astype(BF16)
    from_last = chip_step(last, 1)

    pieces, own, grad_b = pl.pallas_call(
        functools.partial(last_sum, scale),
        out_shape=(
            pltpu.HBM((2 * ys * parts, 8, BLOCK), F32),
            pltpu.HBM(own.shape, F32),
            jax.ShapeDtypeStruct((1, out_feat), F32),
        ),
        in_specs=[VMEM, HBM, ANY, ANY],
        out_specs=(HBM, HBM, VMEM),
        scratch_shapes=[pltpu.VMEM((2 * ys * parts, 8, BLOCK), F32), dma((1,))],
        input_output_aliases={1: 1},
        compiler_params=PARAMS,
        name="last_sum",
    )(partial, *in_hbm(own), last, from_first)
    pieces = lax.all_to_all(pieces, ("y", "c", "x"), 0, 0)

    grad_x, token = pl.pallas_call(
        out_of_order,
        out_shape=(slab, jax.ShapeDtypeStruct((8, BLOCK), F32)),
        in_specs=[HBM] * 2 + [ANY] * 3,
        out_specs=(VMEM, VMEM),
        scratch_shapes=[
            pltpu.VMEM((1, nodes), jnp.int32),
            pltpu.VMEM((nblocks, feat, BLOCK), F32),
            pltpu.VMEM((nblocks, feat, BLOCK), BF16),
            pltpu.VMEM((nblocks, feat, BLOCK), BF16),
            pltpu.VMEM((nblocks, feat, BLOCK), BF16),
            pltpu.VMEM((feat, nodes), BF16),
            dma((5,)),
        ],
        compiler_params=PARAMS,
        cost_estimate=cost(3 * 10**9, 2**21),
        name="out_of_order",
    )(*in_hbm(node_order, own), from_first, pair, from_last)

    grad_w = pl.pallas_call(
        functools.partial(put_together, parts),
        out_shape=jax.ShapeDtypeStruct((parts * 8 * ys, 2 * BLOCK), F32),
        in_specs=[VMEM, ANY],
        out_specs=VMEM,
        compiler_params=PARAMS,
        name="put_together",
    )(pieces, token)
    return output, grad_x, grad_w, grad_b.reshape(out_feat)


def solution(mesh):
    rows, cols = mesh.devices.shape
    ys = 8 if rows % 16 == 0 else 2
    devices = mesh.devices.reshape(rows // (2 * ys), ys, 2, cols)
    own = Mesh(devices, ("z", "y", "c", "x"))
    in_specs = (
        P("x", ROWS),
        P(ROWS, None),
        P(ROWS, None, None),
        P(ROWS, None),
        P(ROWS, None),
        P(ROWS),
        P(),
        P(),
        P(None, ROWS + ("x",)),
    )
    out_specs = (P(None, ROWS + ("x",)), P("x", ROWS), P(), P())
    return jax.shard_map(
        on_device, mesh=own, in_specs=in_specs, out_specs=out_specs, check_vma=False
    )
```

```python
import functools
import math

import jax
import jax.numpy as jnp
from jax import lax
from jax.experimental import pallas as pl
from jax.experimental.pallas import tpu as pltpu
from jax.sharding import Mesh, PartitionSpec as P

BF16 = jnp.bfloat16
F32 = jnp.float32
BLOCK = 128
TILE = 256
ROWS = ("z", "y", "c")
CHUNK = 8
SPAN = 48
VMEM = pl.BlockSpec(memory_space=pltpu.VMEM)
SMEM = pl.BlockSpec(memory_space=pltpu.SMEM)
HBM = pl.BlockSpec(memory_space=pltpu.HBM)
ANY = pl.BlockSpec(memory_space=pl.ANY)
PARAMS = pltpu.CompilerParams(vmem_limit_bytes=40 * 1024 * 1024)


def in_hbm(*arrays):
    return tuple(pltpu.with_memory_space_constraint(array, pltpu.HBM) for array in arrays)


def in_smem(*arrays):
    return tuple(pltpu.with_memory_space_constraint(array, pltpu.SMEM) for array in arrays)


def cost(flops, size):
    return pl.CostEstimate(flops=flops, bytes_accessed=size, transcendentals=0)


def started(pairs, sems):
    copies = [pltpu.make_async_copy(a, b, sems.at[i]) for i, (a, b) in enumerate(pairs)]
    for copy in copies:
        copy.start()
    return copies


def split(index, size):
    return index >> (size.bit_length() - 1), index & (size - 1)


def into_order(order_hbm, x_hbm, adj_hbm, out_ref, adj_ref, order, x, sems):
    copies = started([(x_hbm, x), (order_hbm, order), (adj_hbm, adj_ref)], sems)
    copies[0].wait()
    copies[1].wait()
    count = x.shape[1]
    for start in range(0, count, TILE):
        group, lane = split(order[:, start : start + TILE], BLOCK)
        rows = lax.broadcasted_iota(jnp.int32, (BLOCK, TILE), 0)
        hot = jnp.where(lane == rows, 1.0, 0.0).astype(BF16)
        moved = jnp.zeros((x.shape[0], TILE), F32)
        for g in range(count // BLOCK):
            part = jnp.dot(x[:, g * BLOCK : (g + 1) * BLOCK], hot, preferred_element_type=F32)
            moved = jnp.where(group == g, part, moved)
        out_ref[:, start : start + TILE] = moved.astype(BF16)
    copies[2].wait()


def out_of_order(
    order_hbm, own_hbm, first_hbm, pair_hbm, last_hbm, out_ref, token_ref, order, own, first, near, last, total, stacked, sems
):
    copies = started(
        [
            (last_hbm, last),
            (first_hbm, first),
            (pair_hbm.at[1], near),
            (own_hbm, own),
            (order_hbm, order),
        ],
        sems,
    )
    token_ref[...] = jnp.zeros_like(token_ref)
    for copy in copies:
        copy.wait()
    for block in range(own.shape[0]):
        sums = own[block] + near[block].astype(F32)
        sums = sums + first[block].astype(F32) + last[block].astype(F32)
        total[:, block * BLOCK : (block + 1) * BLOCK] = sums.astype(BF16)
    rows, count = total.shape
    group, lane = split(order[...], BLOCK)
    ids = lax.broadcasted_iota(jnp.int32, (BLOCK, count), 0)
    hot = jnp.where(lane == ids, 1.0, 0.0).astype(BF16)
    group = jnp.broadcast_to(group.astype(F32).astype(BF16), (rows, count))
    values = total[...]
    for g in range(count // BLOCK):
        chosen = jnp.where(group == jnp.asarray(g, BF16), values, jnp.zeros_like(values))
        stacked[g * rows : (g + 1) * rows, :] = chosen
    moved = lax.dot_general(
        stacked[...], hot, (((1,), (1,)), ((), ())), preferred_element_type=F32
    ).astype(BF16)
    for g in range(count // BLOCK):
        out_ref[:, g * BLOCK : (g + 1) * BLOCK] = moved[g * rows : (g + 1) * rows]


def sum_to_all(recv, first_hbm, token, out_hbm, kept_hbm, out, sems):
    total = jnp.sum(recv[...], axis=0)
    for i in range(out.shape[0]):
        out[i] = total
    started([(out, out_hbm)], sems)[0].wait()


def last_sum(scale, recv, own_hbm, token, out_hbm, kept_hbm, bias_ref, out, sems):
    total = jnp.sum(recv[...], axis=0) * scale
    for i in range(out.shape[0]):
        out[i] = total[0:8]
    copies = started([(out, out_hbm)], sems)
    bias_ref[:, 0:BLOCK] = total[8:9]
    bias_ref[:, BLOCK:] = total[12:13]
    copies[0].wait()


def kept(recv, token, out_ref):
    out_ref[...] = recv[...]


def put_together(parts, recv, out_ref):
    rows = out_ref.shape[0] // parts
    for c in range(recv.shape[0]):
        for i in range(recv.shape[1]):
            row, lane = i % parts * rows + 8 * (i // parts), c * BLOCK
            out_ref[row : row + 8, lane : lane + BLOCK] = recv[c, i]


def mirrored(source, core, nblocks, spread):
    offset, block = split(source, nblocks)
    return jnp.where(core == 0, offset, spread - 1 - offset) * nblocks + block


def turned(adj, out_ref):
    for j in range(adj.shape[0]):
        out_ref[j] = adj[j].T


def aggregate(
    count_ref, dest, src, beside, across, permuted, before, after, adj, out_ref, win, acc
):
    slots = adj.shape[0]
    nblocks = acc.shape[0] - 1
    spread = win.shape[0] // nblocks
    quarter = out_ref.shape[2] // BLOCK
    acc[...] = jnp.zeros_like(acc)
    for block in range(nblocks):
        lane = slice(block * BLOCK, (block + 1) * BLOCK)
        win[block] = before[:, lane]
        win[nblocks + block] = across[:, lane]
        win[2 * nblocks + block] = permuted[:, lane]
        win[3 * nblocks + block] = beside[:, lane]
        win[4 * nblocks + block] = after[:, lane]
    core = lax.axis_index("c")
    count = count_ref[0]
    for begin in range(0, slots, CHUNK):
        products = []
        for j in range(begin, begin + CHUNK):
            place = mirrored(src[0, j], core, nblocks, spread)
            products.append(
                jnp.dot(win[place], adj[j], preferred_element_type=F32)
            )
        for j, product in zip(range(begin, begin + CHUNK), products):
            target = jnp.where(j < count, dest[0, j], nblocks)
            acc[target] += product
    for block in range(nblocks):
        lane = (block % quarter) * BLOCK
        out_ref[block // quarter, :, lane : lane + BLOCK] = acc[block].astype(BF16)


def dense(hidden_ref, weight_hbm, bias_hbm, cot_hbm, out_ref, send_ref, weight_v, bias_v, cot, sems):
    copies = started([(weight_hbm, weight_v), (bias_hbm, bias_v), (cot_hbm, cot)], sems)
    feat, width = hidden_ref.shape
    part = send_ref.shape[0]
    rows = feat // part
    hidden = hidden_ref[...]
    copies[0].wait()
    copies[1].wait()
    weight = weight_v[...]
    bias = jnp.broadcast_to(bias_v[...], (BLOCK, bias_v.shape[1])).T
    bias = jnp.concatenate([bias] * (width // BLOCK), axis=1)
    v = (
        lax.dot_general(weight, hidden, (((0,), (0,)), ((), ())), preferred_element_type=F32)
        + bias
    )
    root = math.sqrt(2.0 / math.pi)
    square = v * v
    t = jnp.tanh(root * (v + 0.044715 * (square * v)))
    half = 0.5 * (1.0 + t)
    out_ref[...] = (v * half).astype(BF16)
    slope = half + (0.5 * root) * v * (1.0 - t * t) * (1.0 + (3.0 * 0.044715) * square)
    copies[2].wait()
    grad = (cot[...].astype(F32) * slope).astype(BF16)
    back = jnp.dot(weight, grad, preferred_element_type=F32).astype(BF16)
    grad_w = lax.dot_general(hidden, grad, (((1,), (1,)), ((), ())), preferred_element_type=F32)
    ones = jnp.ones((16, width), BF16)
    grad_b = lax.dot_general(ones, grad, (((1,), (1,)), ((), ())), preferred_element_type=F32)
    high_w = grad_w.astype(BF16)
    low_w = (grad_w - high_w.astype(F32)).astype(BF16)
    high_b = grad_b.astype(BF16)
    low_b = (grad_b - high_b.astype(F32)).astype(BF16)
    half_width = grad_w.shape[1]
    for i in range(part):
        span = slice(i * rows, (i + 1) * rows)
        send_ref[i, 0:rows, :] = back[span]
        send_ref[i, rows : 2 * rows, 0:half_width] = high_w[span]
        send_ref[i, rows : 2 * rows, half_width:] = low_w[span]
        send_ref[i, 2 * rows :, 0:half_width] = high_b
        send_ref[i, 2 * rows :, half_width:] = low_b


def first_sum(recv, out_hbm, grad_hbm, out, sems):
    rows = grad_hbm.shape[1]
    half_width = recv.shape[2] // 2
    copies = started([(recv.at[:, pl.ds(0, rows), :], grad_hbm)], sems)
    total = jnp.zeros((rows + 16, half_width), F32)
    for i in range(recv.shape[0]):
        total = total + recv[i, rows:, 0:half_width].astype(F32)
        total = total + recv[i, rows:, half_width:].astype(F32)
    for i in range(out.shape[0] // 2):
        for c in range(2):
            lane = slice(c * BLOCK, (c + 1) * BLOCK)
            out[2 * i + c, 0:8, :] = total[8 * i : 8 * i + 8, lane]
            out[2 * i + c, 8:12, :] = total[rows : rows + 4, 0:BLOCK]
            out[2 * i + c, 12:16, :] = total[rows : rows + 4, BLOCK : 2 * BLOCK]
    last = pltpu.make_async_copy(out, out_hbm, sems.at[1])
    last.start()
    copies[0].wait()
    last.wait()


def spread_back(
    count_ref, dest_hbm, src_hbm, grad_hbm, adj_hbm,
    first_hbm, pair_hbm, own_hbm, last_hbm, token_ref,
    dest, src, grad, adj, acc, first, pair, sems, adj_sems,
):
    slots = adj.shape[0]
    quarter = grad.shape[2] // BLOCK
    nblocks = grad.shape[0] * quarter
    spread = (acc.shape[0] - 1) // nblocks
    copies = started(
        [(dest_hbm, dest), (src_hbm, src), (grad_hbm, grad)], sems
    )
    spans = [pl.ds(begin, SPAN) for begin in range(0, slots, SPAN)]
    adj_copies = started([(adj_hbm.at[span], adj.at[span]) for span in spans], adj_sems)
    acc[...] = jnp.zeros_like(acc)
    core = lax.axis_index("c")
    count = count_ref[0]
    for copy in copies:
        copy.wait()
    for index, copy in enumerate(adj_copies):
        copy.wait()
        products = []
        for j in range(index * SPAN, (index + 1) * SPAN):
            part, place = split(dest[0, j], quarter)
            picked = grad[part, :, pl.ds(pl.multiple_of(place * BLOCK, BLOCK), BLOCK)]
            products.append(jnp.dot(picked, adj[j], preferred_element_type=F32))
        for j, product in zip(range(index * SPAN, (index + 1) * SPAN), products):
            place = mirrored(src[0, j], core, nblocks, spread)
            place = jnp.where(j < count, place, spread * nblocks)
            acc[place] += product
    outs = started(
        [
            (acc.at[pl.ds(2 * nblocks, nblocks)], own_hbm),
            (acc.at[pl.ds(4 * nblocks, nblocks)], last_hbm),
        ],
        sems,
    )
    pair[0] = acc[nblocks : 2 * nblocks].astype(BF16)
    pair[1] = acc[3 * nblocks : 4 * nblocks].astype(BF16)
    outs.append(pltpu.make_async_copy(pair, pair_hbm, sems.at[3]))
    outs[-1].start()
    first[...] = acc[0:nblocks].astype(BF16)
    outs.append(pltpu.make_async_copy(first, first_hbm, sems.at[4]))
    outs[-1].start()
    token_ref[...] = jnp.zeros_like(token_ref)
    for copy in outs:
        copy.wait()


def on_device(
    features, node_order, adj_values, blk_dest, blk_src, blk_count, weight, bias, cotangent
):
    feat, nodes = features.shape
    slots = adj_values.shape[0]
    nblocks = nodes // BLOCK
    parts = lax.axis_size("x")
    out_feat, width = cotangent.shape
    shards = lax.axis_size(ROWS)
    ys, zs = lax.axis_size("y"), lax.axis_size("z")
    scale = 1.0 / math.sqrt(nodes * shards)

    def chip_step(value, sign):
        pairs = [(s, (s + (2 * sign if s % 2 == 0 else -2 * sign)) % shards) for s in range(shards)]
        return lax.ppermute(value, ROWS, pairs)

    def sibling(value):
        return lax.ppermute(value, "c", [(0, 1), (1, 0)])

    slab = jax.ShapeDtypeStruct((feat, nodes), BF16)
    dma = pltpu.SemaphoreType.DMA

    permuted, adj = pl.pallas_call(
        into_order,
        out_shape=(slab, jax.ShapeDtypeStruct(adj_values.shape, BF16)),
        in_specs=[HBM] * 3,
        out_specs=(VMEM, VMEM),
        scratch_shapes=[
            pltpu.VMEM((1, nodes), jnp.int32),
            pltpu.VMEM((feat, nodes), BF16),
            dma((3,)),
        ],
        compiler_params=PARAMS,
        cost_estimate=cost(10**9, 2**20),
        name="into_order",
    )(*in_hbm(node_order, features, adj_values))

    adj_turned = pl.pallas_call(
        turned,
        out_shape=jax.ShapeDtypeStruct(adj_values.shape, BF16),
        in_specs=[VMEM],
        out_specs=VMEM,
        compiler_params=PARAMS,
        cost_estimate=cost(2 * 10**9, 2**20),
        name="turned",
    )(adj)
    after = chip_step(permuted, -1)
    before = chip_step(permuted, 1)
    beside = sibling(permuted)
    across = sibling(after)

    hidden = pl.pallas_call(
        aggregate,
        out_shape=jax.ShapeDtypeStruct((parts, feat, width), BF16),
        in_specs=[SMEM] * 3 + [VMEM] * 6,
        out_specs=VMEM,
        scratch_shapes=[
            pltpu.VMEM((5 * nblocks, feat, BLOCK), BF16),
            pltpu.VMEM((nblocks + 1, feat, BLOCK), F32),
        ],
        compiler_params=PARAMS,
        cost_estimate=cost(4 * 10**9, 2**22),
        name="aggregate",
    )(blk_count, *in_smem(blk_dest, blk_src), beside, across, permuted, before, after, adj_turned)

    hidden_rows = lax.all_to_all(hidden, "x", 0, 0).reshape(parts * feat, width)

    output, send = pl.pallas_call(
        dense,
        out_shape=(
            jax.ShapeDtypeStruct((out_feat, width), BF16),
            jax.ShapeDtypeStruct((parts, 2 * feat + 16, width), BF16),
        ),
        in_specs=[VMEM] + [HBM] * 3,
        out_specs=(VMEM, VMEM),
        scratch_shapes=[
            pltpu.VMEM(weight.shape, BF16),
            pltpu.VMEM((1, out_feat), F32),
            pltpu.VMEM((out_feat, width), BF16),
            dma((3,)),
        ],
        compiler_params=PARAMS,
        cost_estimate=cost(10**9, 2**20),
        name="dense",
    )(hidden_rows, *in_hbm(weight, bias[None, :], cotangent))

    recv = lax.all_to_all(send, "x", 0, 0)

    partial, grads = pl.pallas_call(
        first_sum,
        out_shape=(
            pltpu.HBM((2 * ys, 16, BLOCK), F32),
            pltpu.HBM((parts, feat, width), BF16),
        ),
        in_specs=[VMEM],
        out_specs=(HBM, HBM),
        scratch_shapes=[pltpu.VMEM((2 * ys, 16, BLOCK), F32), dma((2,))],
        compiler_params=PARAMS,
        cost_estimate=cost(10**9, 2**20),
        name="first_sum",
    )(recv)
    partial = lax.all_to_all(partial, ("y", "c"), 0, 0)

    first, pair, own, last, token = pl.pallas_call(
        spread_back,
        out_shape=(
            pltpu.HBM((nblocks, feat, BLOCK), BF16),
            pltpu.HBM((2, nblocks, feat, BLOCK), BF16),
            pltpu.HBM((nblocks, feat, BLOCK), F32),
            pltpu.HBM((nblocks, feat, BLOCK), F32),
            jax.ShapeDtypeStruct((8, BLOCK), F32),
        ),
        in_specs=[SMEM] + [HBM] * 4,
        out_specs=(HBM,) * 4 + (VMEM,),
        scratch_shapes=[
            pltpu.SMEM((1, slots), jnp.int32),
            pltpu.SMEM((1, slots), jnp.int32),
            pltpu.VMEM((parts, feat, width), BF16),
            pltpu.VMEM((slots, BLOCK, BLOCK), BF16),
            pltpu.VMEM((5 * nblocks + 1, feat, BLOCK), F32),
            pltpu.VMEM((nblocks, feat, BLOCK), BF16),
            pltpu.VMEM((2, nblocks, feat, BLOCK), BF16),
            dma((5,)),
            dma((slots // SPAN,)),
        ],
        compiler_params=PARAMS,
        cost_estimate=cost(4 * 10**9, 2**22),
        name="spread_back",
    )(blk_count, *in_hbm(blk_dest, blk_src, grads, adj_values))

    partial, first = pl.pallas_call(
        sum_to_all,
        out_shape=(pltpu.HBM((zs, 16, BLOCK), F32), pltpu.HBM(first.shape, BF16)),
        in_specs=[VMEM, HBM, ANY],
        out_specs=(HBM, HBM),
        scratch_shapes=[pltpu.VMEM((zs, 16, BLOCK), F32), dma((1,))],
        input_output_aliases={1: 1},
        compiler_params=PARAMS,
        cost_estimate=cost(3 * 10**10, 2**20),
        name="sum_to_all",
    )(partial, *in_hbm(first), token)
    partial = lax.all_to_all(partial, "z", 0, 0)

    pair = sibling(pair)
    from_first = chip_step(first, -1)
    last = (last + pair[0].astype(F32)).astype(BF16)
    from_last = chip_step(last, 1)

    pieces, own, grad_b = pl.pallas_call(
        functools.partial(last_sum, scale),
        out_shape=(
            pltpu.HBM((ys * parts, 8, BLOCK), F32),
            pltpu.HBM(own.shape, F32),
            jax.ShapeDtypeStruct((1, out_feat), F32),
        ),
        in_specs=[VMEM, HBM, ANY],
        out_specs=(HBM, HBM, VMEM),
        scratch_shapes=[pltpu.VMEM((ys * parts, 8, BLOCK), F32), dma((1,))],
        input_output_aliases={1: 1},
        compiler_params=PARAMS,
        name="last_sum",
    )(partial, *in_hbm(own), last)
    pieces = lax.all_to_all(pieces, ("y", "x"), 0, 0)

    grad_x, token = pl.pallas_call(
        out_of_order,
        out_shape=(slab, jax.ShapeDtypeStruct((8, BLOCK), F32)),
        in_specs=[HBM] * 2 + [ANY] * 3,
        out_specs=(VMEM, VMEM),
        scratch_shapes=[
            pltpu.VMEM((1, nodes), jnp.int32),
            pltpu.VMEM((nblocks, feat, BLOCK), F32),
            pltpu.VMEM((nblocks, feat, BLOCK), BF16),
            pltpu.VMEM((nblocks, feat, BLOCK), BF16),
            pltpu.VMEM((nblocks, feat, BLOCK), BF16),
            pltpu.VMEM((feat, nodes), BF16),
            pltpu.VMEM((nblocks * feat, nodes), BF16),
            dma((5,)),
        ],
        compiler_params=PARAMS,
        cost_estimate=cost(3 * 10**9, 2**21),
        name="out_of_order",
    )(*in_hbm(node_order, own), from_first, pair, from_last)

    pieces = pl.pallas_call(
        kept,
        out_shape=jax.ShapeDtypeStruct(pieces.shape, F32),
        in_specs=[VMEM, ANY],
        out_specs=VMEM,
        compiler_params=PARAMS,
        name="kept",
    )(pieces, token)
    grad_w = pl.pallas_call(
        functools.partial(put_together, parts),
        out_shape=jax.ShapeDtypeStruct((parts * 8 * ys, 2 * BLOCK), F32),
        in_specs=[VMEM],
        out_specs=VMEM,
        compiler_params=PARAMS,
        name="put_together",
    )(lax.all_gather(pieces, "c"))
    return output, grad_x, grad_w, grad_b.reshape(out_feat)


def solution(mesh):
    rows, cols = mesh.devices.shape
    ys = 8 if rows % 16 == 0 else 2
    devices = mesh.devices.reshape(rows // (2 * ys), ys, 2, cols)
    own = Mesh(devices, ("z", "y", "c", "x"))
    in_specs = (
        P("x", ROWS),
        P(ROWS, None),
        P(ROWS, None, None),
        P(ROWS, None),
        P(ROWS, None),
        P(ROWS),
        P(),
        P(),
        P(None, ROWS + ("x",)),
    )
    out_specs = (P(None, ROWS + ("x",)), P("x", ROWS), P(), P())
    return jax.shard_map(
        on_device, mesh=own, in_specs=in_specs, out_specs=out_specs, check_vma=False
    )
```
